128 devices in a mesh: depth: 2 (over core), lat: 64 (over z, y, x).
Axes of the slice: x: 4, y: 4, z: 4, core: 2. Of those that a mesh axis runs over, the one named last changes fastest.
Arguments:
- transmission: float32 [2, 4, 4096, 1024], P(None, 'depth', 'lat')
- probe: float32 [2, 128, 128], replicated, may hold values from -6 to 6
- amplitude: float32 [256, 128, 128], P('lat'), may hold values from 0.2 to 3
- positions: int32 [256, 2], P('lat'), may hold values from 0 to 4095, as said below
- counts: int32 [64], P('lat'), may hold values from 1 to 4, as said below
Outputs:
- gradient: float32 [2, 4, 4096, 1024], P(None, 'depth', 'lat')
The draws below stay inside these ranges and needn't reach their ends.
Inputs may be any that keep to these rules, and one draw needn't show every extreme that they name: positions[p][0] lies in the rows of tile p // 4, that is between (p // 4) * 64 and (p // 4 + 1) * 64 - 1; positions[p][1] is a column of the object; every slot, live or not, holds such a position. `counts`: the largest count is 4.
All inputs are finite; a program needn't handle non-finite values.
Results may differ from the reference program's by a relative error of at most 0.0003.
Values sent between devices are 32-bit elements; how exact they have to be, the bound alone decides.
A program may use at most 64 MiB of HBM per device.

```python
import math
import jax
import jax.numpy as jnp
from jax import lax

WIN = 128
STRIP = 64
COLS = 1024
CAP = 4
SLICES = 4
ROWS = 4096
TILES = 64
POSITIONS = 256


def draw_transmission(key, part):
    key = jax.random.fold_in(key, 11)
    key_re, key_im = jax.random.split(key)
    shape = (SLICES, ROWS, COLS)
    real_part = jax.random.uniform(key_re, shape, jnp.float32, 0.8, 1.15)
    imag_part = jax.random.uniform(key_im, shape, jnp.float32, -0.3, 0.3)
    return jnp.stack([real_part, imag_part]).astype(jnp.float32)


def draw_positions(key, part):
    key = jax.random.fold_in(key, 12)
    key_row, key_col = jax.random.split(key)
    tile = jnp.arange(POSITIONS, dtype=jnp.int32) // CAP
    rows = tile * STRIP + jax.random.randint(key_row, (POSITIONS,), 0, STRIP, jnp.int32)
    cols = jax.random.randint(key_col, (POSITIONS,), 0, COLS, jnp.int32)
    return jnp.stack([rows, cols], axis=1).astype(jnp.int32)


def draw_counts(key, part):
    key = jax.random.fold_in(key, 13)
    key_pick, key_base = jax.random.split(key)
    pick = jax.random.randint(key_pick, (TILES,), 0, 5, jnp.int32)
    base = jax.random.randint(key_base, (TILES,), 1, 3, jnp.int32)
    result = jnp.where(pick == 0, CAP, jnp.minimum(base, CAP))
    result = result.at[0].set(CAP)
    return result.astype(jnp.int32)


def shard_levels(rng, dims, pieces, smallest, largest):
    factor_of = 1.0
    for axis_at, shards_of in pieces:
        draws = jax.random.uniform(jax.random.fold_in(jax.random.fold_in(rng, 6), axis_at), (shards_of,), jnp.float32, smallest / len(pieces), largest / len(pieces))
        factor_of = factor_of * jnp.repeat(jnp.exp(draws), dims[axis_at] // shards_of).reshape((-1,) + (1,) * (len(dims) - 1 - axis_at))
    return factor_of


def scatter_about(own_key, dims, scale, bound, kind=jnp.bfloat16):
    drawn = scale * jax.random.normal(own_key, dims, jnp.float32)
    return jnp.clip(drawn, min=-bound, max=bound).astype(kind)


def setup_inputs(seed: int = 0) -> dict:
    key_list = jax.random.split(jax.random.key(seed), 6)
    return {
        "transmission": draw_transmission(jax.random.fold_in(key_list[5], 71), 0),
        "probe": scatter_about(key_list[1], (2, WIN, WIN), 1.0, 6.0, jnp.float32),
        "amplitude": jnp.clip(jnp.exp(math.log(3.0) - 2.7080502 * jax.random.uniform(key_list[2], (POSITIONS, WIN, WIN), jnp.float32) ** shard_levels(key_list[2], (POSITIONS, WIN, WIN), ((0, 64),), -0.2, 0.2)), 0.2, 3.0),
        "positions": draw_positions(jax.random.fold_in(key_list[5], 71), 0),
        "counts": draw_counts(jax.random.fold_in(key_list[5], 71), 0),
    }


PROP_COEF = 40.0

def propagator(width):
    index = jnp.arange(width, dtype=jnp.int32)
    signed = (index + width // 2) % width - width // 2
    freq = signed.astype(jnp.float32) / width
    phase = -PROP_COEF * (freq[:, None] * freq[:, None] + freq[None, :] * freq[None, :])
    return (jnp.cos(phase), jnp.sin(phase))

def forward_two(x):
    return jnp.fft.fft2(x, norm='ortho')

def inverse_two(x):
    return jnp.fft.ifft2(x, norm='ortho')

def reference(transmission, probe, amplitude, positions, counts):
    width = WIN
    half = width // 2
    padded = jnp.pad(transmission, ((0, 0), (0, 0), (half, half), (half, half)))
    prop_re, prop_im = propagator(width)
    kernel = lax.complex(prop_re, prop_im)
    probe_wave = lax.complex(probe[0], probe[1])
    slot_ids = jnp.arange(POSITIONS, dtype=jnp.int32)
    live = (slot_ids % CAP < counts[slot_ids // CAP]).astype(jnp.float32)

    def one_slot(grad, inputs):
        centre, measured, alive = inputs
        start = (jnp.int32(0), jnp.int32(0), centre[0].astype(jnp.int32), centre[1].astype(jnp.int32))
        window = lax.dynamic_slice(padded, start, (2, SLICES, width, width))
        trans = lax.complex(window[0], window[1])

        def forward(psi, slab):
            return (inverse_two(kernel * forward_two(psi * slab)), psi)
        exit_wave, befores = lax.scan(forward, probe_wave, trans)
        far = forward_two(exit_wave)
        magnitude = jnp.sqrt(far.real * far.real + far.imag * far.imag + 1.0)
        weight = alive * (magnitude - measured) / magnitude
        chi = inverse_two(weight * far)

        def backward(carry, inputs_back):
            slab, before = inputs_back
            back = inverse_two(jnp.conj(kernel) * forward_two(carry))
            return (jnp.conj(slab) * back, jnp.conj(before) * back)
        _, terms = lax.scan(backward, chi, (trans, befores), reverse=True)
        piece = jnp.stack([terms.real, terms.imag])
        current = lax.dynamic_slice(grad, start, (2, SLICES, width, width))
        grad = lax.dynamic_update_slice(grad, current + piece, start)
        return (grad, None)
    grad = jnp.zeros(padded.shape, jnp.float32)
    grad, _ = lax.scan(one_slot, grad, (positions, amplitude, live))
    return grad[:, :, half:half + ROWS, half:half + COLS]
```

```python
import functools

import jax
import jax.numpy as jnp
import ml_dtypes
import numpy as np
from jax import lax
from jax.experimental import pallas as pl
from jax.experimental.pallas import tpu as pltpu
from jax.sharding import PartitionSpec as P

PROP_COEF = 40.0
WIN = 128
HALF = 64
MESH = pl.DeviceIdType.MESH
PROP, PROP_CONJ, DFT, DFT_CONJ = range(4)


def tables():
    index = np.arange(WIN)
    dft = np.exp(-2j * np.pi * (np.outer(index, index) % WIN) / WIN) / np.sqrt(WIN)
    freq = ((index + WIN // 2) % WIN - WIN // 2) / WIN
    prop = dft.conj() @ np.diag(np.exp(-1j * PROP_COEF * freq * freq)) @ dft
    terms = []
    for matrix in (prop, prop.conj(), dft, dft.conj()):
        real = np.block([[matrix.real, -matrix.imag], [matrix.imag, matrix.real]])
        high = real.astype(ml_dtypes.bfloat16)
        low = (real - high.astype(np.float64)).astype(ml_dtypes.bfloat16)
        terms.append(np.stack([high, low]))
    return np.stack(terms)


def split(values):
    high = values.astype(jnp.bfloat16)
    low = (values - high.astype(jnp.float32)).astype(jnp.bfloat16)
    return high, low


def product(mats, which, re, im):
    conj = which ^ 1
    high, low = split(jnp.concatenate([re, im], axis=1))
    right = jnp.concatenate([mats[conj, 0], mats[conj, 0], mats[conj, 1]], axis=0)
    first = jnp.dot(
        jnp.concatenate([high, low, high], axis=1), right, preferred_element_type=jnp.float32
    )
    high, low = split(jnp.concatenate([first[:, :WIN], first[:, WIN:]], axis=0))
    left = jnp.concatenate([mats[which, 0], mats[which, 0], mats[which, 1]], axis=1)
    second = jnp.dot(
        left, jnp.concatenate([high, low, high], axis=0), preferred_element_type=jnp.float32
    )
    return second[:WIN], second[WIN:]


def column_block(pos, slot):
    column = pos[slot, 1] + HALF
    return lax.shift_right_logical(column, 7), column & (WIN - 1)


def cut(tile, pos, slot):
    block, lane = column_block(pos, slot)
    lanes = lax.broadcasted_iota(jnp.int32, (2, 2, HALF, WIN), 3)
    return jnp.where(lanes >= lane, tile[block], tile[block + 1])


def kernel(
    n, pos, counts, trans, probe, amp, mats_hbm,
    from_prev, from_next, own, pos_prev_out, pos_next_out,
    tile, mats, to_prev, to_next, have_prev, have_next, window, waves,
    wave_out, wave_in, top, bottom, pos_prev, pos_next,
    tile_sem, mats_sem, pos_send, pos_recv, win_send, win_recv, wave_send, wave_recv,
    grad_send, grad_recv, own_sem,
):
    core = lax.axis_index("depth")
    lat = lax.axis_index("lat")
    has_prev = lat > 0
    has_next = lat < n - 1
    slots = pos.shape[0]
    blocks = tile.shape[0] - 2
    partner = (1 - core, lat)
    sides = ((0, has_prev, (core, lat - 1)), (1, has_next, (core, lat + 1)))

    loads = [
        pltpu.make_async_copy(
            trans.at[:, :, :, pl.ds(k * WIN, WIN)], tile.at[k + 1], tile_sem.at[k]
        )
        for k in range(blocks)
    ]
    for load in loads:
        load.start()
    mats_load = pltpu.make_async_copy(mats_hbm, mats, mats_sem)
    mats_load.start()

    barrier = pltpu.get_barrier_semaphore()
    pl.semaphore_signal(barrier, inc=1, device_id=partner, device_id_type=MESH)
    for _, there, device in sides:
        @pl.when(there)
        def _():
            pl.semaphore_signal(barrier, inc=1, device_id=device, device_id_type=MESH)

    tile[0] = jnp.zeros(tile.shape[1:], jnp.float32)
    tile[blocks + 1] = jnp.zeros(tile.shape[1:], jnp.float32)

    @pl.when(jnp.logical_not(has_prev))
    def _():
        have_prev[...] = jnp.zeros_like(have_prev)
        for k in range(4):
            pos_prev[k, 0] = 0
            pos_prev[k, 1] = 0

    @pl.when(jnp.logical_not(has_next))
    def _():
        have_next[...] = jnp.zeros_like(have_next)
        for k in range(4):
            pos_next[k, 0] = 0
            pos_next[k, 1] = 0

    pl.semaphore_wait(barrier, 1 + has_prev.astype(jnp.int32) + has_next.astype(jnp.int32))

    def pos_copy(side, device):
        landing = (pos_next, pos_prev)[side]
        return pltpu.make_async_remote_copy(
            src_ref=pos, dst_ref=landing, send_sem=pos_send.at[side], recv_sem=pos_recv.at[1 - side],
            device_id=device, device_id_type=MESH,
        )

    def pos_arrival(side, device):
        landing = (pos_prev, pos_next)[side]
        return pltpu.make_async_remote_copy(
            src_ref=pos, dst_ref=landing, send_sem=pos_send.at[side], recv_sem=pos_recv.at[side],
            device_id=device, device_id_type=MESH,
        )

    def win_copy(side, slot, device):
        source = (to_prev, to_next)[side]
        landing = (have_next, have_prev)[side]
        return pltpu.make_async_remote_copy(
            src_ref=source.at[slot], dst_ref=landing.at[slot],
            send_sem=win_send.at[side, slot], recv_sem=win_recv.at[1 - side, slot],
            device_id=device, device_id_type=MESH,
        )

    def win_arrival(side, slot, device):
        landing = (have_prev, have_next)[side]
        return pltpu.make_async_remote_copy(
            src_ref=to_prev.at[slot], dst_ref=landing.at[slot],
            send_sem=win_send.at[side, slot], recv_sem=win_recv.at[side, slot],
            device_id=device, device_id_type=MESH,
        )

    def grad_copy(side, slot, device):
        landing = (from_next, from_prev)[side]
        return pltpu.make_async_remote_copy(
            src_ref=top.at[slot], dst_ref=landing.at[slot],
            send_sem=grad_send.at[side, slot], recv_sem=grad_recv.at[1 - side, slot],
            device_id=device, device_id_type=MESH,
        )

    def grad_arrival(side, slot, device):
        landing = (from_prev, from_next)[side]
        return pltpu.make_async_remote_copy(
            src_ref=top.at[slot], dst_ref=landing.at[slot],
            send_sem=grad_send.at[side, slot], recv_sem=grad_recv.at[side, slot],
            device_id=device, device_id_type=MESH,
        )

    def wave_copy(slot):
        return pltpu.make_async_remote_copy(
            src_ref=wave_out.at[slot], dst_ref=wave_in.at[slot],
            send_sem=wave_send.at[slot], recv_sem=wave_recv.at[slot],
            device_id=partner, device_id_type=MESH,
        )

    def own_copy(slot):
        return pltpu.make_async_copy(bottom.at[slot], own.at[slot], own_sem.at[slot])

    for side, there, device in sides:
        @pl.when(there)
        def _():
            pos_copy(side, device).start()

    for load in loads:
        load.wait()
    for side, there, device in sides:
        @pl.when(there)
        def _():
            pos_arrival(side, device).wait_recv()

    def send_windows(slot, carry):
        for side, there, device in sides:
            buffer = (to_prev, to_next)[side]
            theirs = (pos_prev, pos_next)[side]

            @pl.when(there)
            def _():
                buffer[slot] = cut(tile, theirs, slot)
                win_copy(side, slot, device).start()

        return carry

    lax.fori_loop(0, slots, send_windows, 0)

    def build_window(slot):
        for side, there, device in sides:
            @pl.when(there)
            def _():
                win_arrival(side, slot, device).wait_recv()

        row = pos[slot, 0] - lat * HALF
        rows = lax.broadcasted_iota(jnp.int32, (2, 2, HALF, WIN), 2)
        window[slot, :, :, :HALF] = jnp.where(rows >= row, have_prev[slot], have_next[slot])
        window[slot, :, :, HALF:] = cut(tile, pos, slot)

    def times(slot, layer, re, im):
        t_re, t_im = window[slot, 0, layer], window[slot, 1, layer]
        return re * t_re - im * t_im, re * t_im + im * t_re

    def times_conj(slot, layer, re, im):
        t_re, t_im = window[slot, 0, layer], window[slot, 1, layer]
        return re * t_re + im * t_im, im * t_re - re * t_im

    def store_term(slot, layer, re, im):
        p_re, p_im = waves[slot, layer, 0], waves[slot, layer, 1]
        term_re = p_re * re + p_im * im
        term_im = p_re * im - p_im * re
        top[slot, 0, layer] = term_re[:HALF]
        top[slot, 1, layer] = term_im[:HALF]
        bottom[slot, 0, layer] = term_re[HALF:]
        bottom[slot, 1, layer] = term_im[HALF:]

    def send_terms(slot):
        for side, there, device in sides:
            @pl.when(there)
            def _():
                grad_copy(side, slot, device).start()

        own_copy(slot).start()

    mats_load.wait()

    @pl.when(core == 0)
    def _():
        def forward(slot):
            build_window(slot)
            row = pos[slot, 0] - lat * HALF
            _, lane = column_block(pos, slot)
            re = pltpu.roll(pltpu.roll(probe[0], row, 0), lane, 1)
            im = pltpu.roll(pltpu.roll(probe[1], row, 0), lane, 1)
            waves[slot, 0, 0] = re
            waves[slot, 0, 1] = im
            re, im = product(mats, PROP, *times(slot, 0, re, im))
            waves[slot, 1, 0] = re
            waves[slot, 1, 1] = im
            re, im = product(mats, PROP, *times(slot, 1, re, im))
            wave_out[slot, 0] = re
            wave_out[slot, 1] = im
            wave_copy(slot).start()

        def backward(slot):
            wave_copy(slot).wait_recv()
            re, im = product(mats, PROP_CONJ, wave_in[slot, 0], wave_in[slot, 1])
            store_term(slot, 1, re, im)
            re, im = product(mats, PROP_CONJ, *times_conj(slot, 1, re, im))
            store_term(slot, 0, re, im)
            send_terms(slot)

        def step(at, carry):
            @pl.when(at < slots)
            def _():
                forward(at)

            @pl.when(at >= 2)
            def _():
                backward(at - 2)

            return carry

        lax.fori_loop(0, slots + 2, step, 0)

    @pl.when(core == 1)
    def _():
        def whole(slot, carry):
            build_window(slot)
            wave_copy(slot).wait_recv()
            re, im = wave_in[slot, 0], wave_in[slot, 1]
            waves[slot, 0, 0] = re
            waves[slot, 0, 1] = im
            re, im = product(mats, PROP, *times(slot, 0, re, im))
            waves[slot, 1, 0] = re
            waves[slot, 1, 1] = im
            re, im = product(mats, DFT, *times(slot, 1, re, im))
            live = jnp.where(slot < counts[0], 1.0, 0.0).astype(jnp.float32)
            weight = live * (1.0 - amp[slot] / jnp.sqrt(re * re + im * im + 1.0))
            re, im = product(mats, DFT_CONJ, weight * re, weight * im)
            store_term(slot, 1, re, im)
            re, im = product(mats, PROP_CONJ, *times_conj(slot, 1, re, im))
            store_term(slot, 0, re, im)
            re, im = times_conj(slot, 0, re, im)
            wave_out[slot, 0] = re
            wave_out[slot, 1] = im
            wave_copy(slot).start()
            send_terms(slot)
            return carry

        lax.fori_loop(0, slots, whole, 0)

    for k in range(4):
        pos_prev_out[k, 0] = pos_prev[k, 0]
        pos_prev_out[k, 1] = pos_prev[k, 1]
        pos_next_out[k, 0] = pos_next[k, 0]
        pos_next_out[k, 1] = pos_next[k, 1]

    def finish(slot, carry):
        own_copy(slot).wait()
        wave_copy(slot).wait_send()
        for side, there, device in sides:
            @pl.when(there)
            def _():
                win_copy(side, slot, device).wait_send()
                grad_copy(side, slot, device).wait_send()
                grad_arrival(side, slot, device).wait_recv()

        return carry

    for side, there, device in sides:
        @pl.when(there)
        def _():
            pos_copy(side, device).wait_send()

    lax.fori_loop(0, slots, finish, 0)


def place_kernel(n, pos, pos_prev, pos_next, own, from_prev, from_next, out, sums):
    lat = lax.axis_index("lat")
    blocks = sums.shape[0] - 2
    sums[...] = jnp.zeros_like(sums)
    shape = (2, 2, HALF, WIN)
    rows = lax.broadcasted_iota(jnp.int32, shape, 2)
    lanes = lax.broadcasted_iota(jnp.int32, shape, 3)

    def add(where, slot, piece, keep):
        block, lane = column_block(where, slot)
        if keep is not None:
            piece = jnp.where(keep, piece, 0.0)
        sums[block] += jnp.where(lanes >= lane, piece, 0.0)
        sums[block + 1] += jnp.where(lanes >= lane, 0.0, piece)

    def one(slot, carry):
        add(pos, slot, own[slot], None)

        @pl.when(lat > 0)
        def _():
            row = pos_prev[slot, 0] - (lat - 1) * HALF
            add(pos_prev, slot, from_prev[slot], rows < row)

        @pl.when(lat < n - 1)
        def _():
            row = pos_next[slot, 0] - (lat + 1) * HALF
            add(pos_next, slot, from_next[slot], rows >= row)

        return carry

    lax.fori_loop(0, pos.shape[0], one, 0)
    for k in range(blocks):
        out[:, :, :, k * WIN : (k + 1) * WIN] = sums[k + 1]


def on_device(n, trans, probe, amp, pos, counts):
    slots = pos.shape[0]
    blocks = trans.shape[3] // WIN
    smem = pl.BlockSpec(memory_space=pltpu.SMEM)
    vmem = pl.BlockSpec(memory_space=pltpu.VMEM)
    any_space = pl.BlockSpec(memory_space=pl.ANY)
    piece = (slots, 2, 2, HALF, WIN)
    wave = (slots, 2, WIN, WIN)
    f32 = jnp.float32
    mats = jnp.asarray(tables())
    from_prev, from_next, own, pos_prev, pos_next = pl.pallas_call(
        functools.partial(kernel, n),
        out_shape=[jax.ShapeDtypeStruct(piece, f32)] * 3 + [jax.ShapeDtypeStruct(pos.shape, jnp.int32)] * 2,
        in_specs=[smem, smem, any_space, vmem, vmem, any_space],
        out_specs=[any_space, any_space, any_space, smem, smem],
        scratch_shapes=[
            pltpu.VMEM((blocks + 2, 2, 2, HALF, WIN), f32),
            pltpu.VMEM(mats.shape, jnp.bfloat16),
            pltpu.VMEM(piece, f32),
            pltpu.VMEM(piece, f32),
            pltpu.VMEM(piece, f32),
            pltpu.VMEM(piece, f32),
            pltpu.VMEM((slots, 2, 2, WIN, WIN), f32),
            pltpu.VMEM((slots, 2, 2, WIN, WIN), f32),
            pltpu.VMEM(wave, f32),
            pltpu.VMEM(wave, f32),
            pltpu.VMEM(piece, f32),
            pltpu.VMEM(piece, f32),
            pltpu.SMEM(pos.shape, jnp.int32),
            pltpu.SMEM(pos.shape, jnp.int32),
            pltpu.SemaphoreType.DMA((blocks,)),
            pltpu.SemaphoreType.DMA(()),
            pltpu.SemaphoreType.DMA((2,)),
            pltpu.SemaphoreType.DMA((2,)),
            pltpu.SemaphoreType.DMA((2, slots)),
            pltpu.SemaphoreType.DMA((2, slots)),
            pltpu.SemaphoreType.DMA((slots,)),
            pltpu.SemaphoreType.DMA((slots,)),
            pltpu.SemaphoreType.DMA((2, slots)),
            pltpu.SemaphoreType.DMA((2, slots)),
            pltpu.SemaphoreType.DMA((slots,)),
        ],
        compiler_params=pltpu.CompilerParams(
            collective_id=0, has_side_effects=True, vmem_limit_bytes=40 << 20
        ),
        name="windows",
    )(pos, counts, trans, probe, amp, mats)
    return pl.pallas_call(
        functools.partial(place_kernel, n),
        out_shape=jax.ShapeDtypeStruct(trans.shape, f32),
        in_specs=[smem, smem, smem, vmem, vmem, vmem],
        out_specs=vmem,
        scratch_shapes=[pltpu.VMEM((blocks + 2, 2, 2, HALF, WIN), f32)],
        compiler_params=pltpu.CompilerParams(vmem_limit_bytes=40 << 20),
        name="place",
    )(pos, pos_prev, pos_next, own, from_prev, from_next)


def solution(mesh):
    placed = (P(None, "depth", "lat", None), P(), P("lat", None, None), P("lat", None), P("lat"))
    return jax.shard_map(
        functools.partial(on_device, mesh.shape["lat"]),
        mesh=mesh,
        in_specs=placed,
        out_specs=P(None, "depth", "lat", None),
        check_vma=False,
    )
```

```python
import functools

import jax
import jax.numpy as jnp
import ml_dtypes
import numpy as np
from jax import lax
from jax.experimental import pallas as pl
from jax.experimental.pallas import tpu as pltpu
from jax.sharding import PartitionSpec as P

PROP_COEF = 40.0
WIN = 128
HALF = 64
MESH = pl.DeviceIdType.MESH
PROP, PROP_CONJ, DFT, DFT_CONJ = range(4)


def tables():
    index = np.arange(WIN)
    dft = np.exp(-2j * np.pi * (np.outer(index, index) % WIN) / WIN) / np.sqrt(WIN)
    freq = ((index + WIN // 2) % WIN - WIN // 2) / WIN
    prop = dft.conj() @ np.diag(np.exp(-1j * PROP_COEF * freq * freq)) @ dft
    terms = []
    for matrix in (prop, prop.conj(), dft, dft.conj()):
        real = np.block([[matrix.real, -matrix.imag], [matrix.imag, matrix.real]])
        high = real.astype(ml_dtypes.bfloat16)
        low = (real - high.astype(np.float64)).astype(ml_dtypes.bfloat16)
        terms.append(np.stack([high, low]))
    return np.stack(terms)


def split(values):
    high = values.astype(jnp.bfloat16)
    low = (values - high.astype(jnp.float32)).astype(jnp.bfloat16)
    return high, low


def product(mats, which, re, im):
    conj = which ^ 1
    high, low = split(jnp.concatenate([re, im], axis=1))
    right = jnp.concatenate([mats[conj, 0], mats[conj, 0], mats[conj, 1]], axis=0)
    first = jnp.dot(
        jnp.concatenate([high, low, high], axis=1), right, preferred_element_type=jnp.float32
    )
    high, low = split(jnp.concatenate([first[:, :WIN], first[:, WIN:]], axis=0))
    left = jnp.concatenate([mats[which, 0], mats[which, 0], mats[which, 1]], axis=1)
    second = jnp.dot(
        left, jnp.concatenate([high, low, high], axis=0), preferred_element_type=jnp.float32
    )
    return second[:WIN], second[WIN:]


def column_block(pos, slot):
    column = pos[1, slot] + HALF
    return lax.shift_right_logical(column, 7), column & (WIN - 1)


def cut(tile, pos, slot):
    block, lane = column_block(pos, slot)
    lanes = lax.broadcasted_iota(jnp.int32, (2, 2, HALF, WIN), 3)
    return jnp.where(lanes >= lane, tile[block], tile[block + 1])


def kernel(
    n, pos_hbm, counts_hbm, trans, probe_hbm, amp_hbm, mats_hbm,
    from_prev, from_next, own, pos_out,
    tile, probe, amp, mats, to_prev, to_next, have_prev, have_next, window, waves,
    wave_out, wave_in, top, bottom, pos, counts, pos_prev, pos_next,
    tile_sem, table_sem, pos_sem, pos_send, pos_recv, win_send, win_recv, wave_send, wave_recv,
    grad_send, grad_recv, own_sem,
):
    core = lax.axis_index("depth")
    lat = lax.axis_index("lat")
    has_prev = lat > 0
    has_next = lat < n - 1
    slots = pos.shape[1]
    blocks = tile.shape[0] - 2
    partner = (1 - core, lat)
    sides = ((0, has_prev, (core, lat - 1)), (1, has_next, (core, lat + 1)))

    scalars = [
        pltpu.make_async_copy(source, target, pos_sem.at[k])
        for k, (source, target) in enumerate(((pos_hbm, pos), (counts_hbm, counts)))
    ]
    for load in scalars:
        load.start()
    loads = [
        pltpu.make_async_copy(
            trans.at[:, :, :, pl.ds(k * WIN, WIN)], tile.at[k + 1], tile_sem.at[k]
        )
        for k in range(blocks)
    ]
    for load in loads:
        load.start()
    tables_in = [
        pltpu.make_async_copy(source, target, table_sem.at[k])
        for k, (source, target) in enumerate(((mats_hbm, mats), (probe_hbm, probe), (amp_hbm, amp)))
    ]
    for load in tables_in:
        load.start()

    barrier = pltpu.get_barrier_semaphore()
    pl.semaphore_signal(barrier, inc=1, device_id=partner, device_id_type=MESH)
    for _, there, device in sides:
        @pl.when(there)
        def _():
            pl.semaphore_signal(barrier, inc=1, device_id=device, device_id_type=MESH)

    tile[0] = jnp.zeros(tile.shape[1:], jnp.float32)
    tile[blocks + 1] = jnp.zeros(tile.shape[1:], jnp.float32)

    @pl.when(jnp.logical_not(has_prev))
    def _():
        have_prev[...] = jnp.zeros_like(have_prev)
        for k in range(slots):
            pos_prev[0, k] = 0
            pos_prev[1, k] = 0

    @pl.when(jnp.logical_not(has_next))
    def _():
        have_next[...] = jnp.zeros_like(have_next)
        for k in range(slots):
            pos_next[0, k] = 0
            pos_next[1, k] = 0

    pl.semaphore_wait(barrier, 1 + has_prev.astype(jnp.int32) + has_next.astype(jnp.int32))

    def pos_copy(side, device):
        landing = (pos_next, pos_prev)[side]
        return pltpu.make_async_remote_copy(
            src_ref=pos_hbm, dst_ref=landing, send_sem=pos_send.at[side], recv_sem=pos_recv.at[1 - side],
            device_id=device, device_id_type=MESH,
        )

    def pos_arrival(side, device):
        landing = (pos_prev, pos_next)[side]
        return pltpu.make_async_remote_copy(
            src_ref=pos_hbm, dst_ref=landing, send_sem=pos_send.at[side], recv_sem=pos_recv.at[side],
            device_id=device, device_id_type=MESH,
        )

    def win_copy(side, slot, device):
        source = (to_prev, to_next)[side]
        landing = (have_next, have_prev)[side]
        return pltpu.make_async_remote_copy(
            src_ref=source.at[slot], dst_ref=landing.at[slot],
            send_sem=win_send.at[side, slot], recv_sem=win_recv.at[1 - side, slot],
            device_id=device, device_id_type=MESH,
        )

    def win_arrival(side, slot, device):
        landing = (have_prev, have_next)[side]
        return pltpu.make_async_remote_copy(
            src_ref=to_prev.at[slot], dst_ref=landing.at[slot],
            send_sem=win_send.at[side, slot], recv_sem=win_recv.at[side, slot],
            device_id=device, device_id_type=MESH,
        )

    def grad_copy(side, slot, device):
        landing = (from_next, from_prev)[side]
        return pltpu.make_async_remote_copy(
            src_ref=top.at[slot], dst_ref=landing.at[slot],
            send_sem=grad_send.at[side, slot], recv_sem=grad_recv.at[1 - side, slot],
            device_id=device, device_id_type=MESH,
        )

    def grad_arrival(side, slot, device):
        landing = (from_prev, from_next)[side]
        return pltpu.make_async_remote_copy(
            src_ref=top.at[slot], dst_ref=landing.at[slot],
            send_sem=grad_send.at[side, slot], recv_sem=grad_recv.at[side, slot],
            device_id=device, device_id_type=MESH,
        )

    def wave_copy(slot):
        return pltpu.make_async_remote_copy(
            src_ref=wave_out.at[slot], dst_ref=wave_in.at[slot],
            send_sem=wave_send.at[slot], recv_sem=wave_recv.at[slot],
            device_id=partner, device_id_type=MESH,
        )

    def own_copy(slot):
        return pltpu.make_async_copy(bottom.at[slot], own.at[slot], own_sem.at[slot])

    for side, there, device in sides:
        @pl.when(there)
        def _():
            pos_copy(side, device).start()

    for load in scalars + loads:
        load.wait()
    for side, there, device in sides:
        @pl.when(there)
        def _():
            pos_arrival(side, device).wait_recv()

    def send_windows(slot, carry):
        for side, there, device in sides:
            buffer = (to_prev, to_next)[side]
            theirs = (pos_prev, pos_next)[side]

            @pl.when(there)
            def _():
                buffer[slot] = cut(tile, theirs, slot)
                win_copy(side, slot, device).start()

        return carry

    lax.fori_loop(0, slots, send_windows, 0)

    def build_window(slot):
        for side, there, device in sides:
            @pl.when(there)
            def _():
                win_arrival(side, slot, device).wait_recv()

        row = pos[0, slot] - lat * HALF
        rows = lax.broadcasted_iota(jnp.int32, (2, 2, HALF, WIN), 2)
        window[slot, :, :, :HALF] = jnp.where(rows >= row, have_prev[slot], have_next[slot])
        window[slot, :, :, HALF:] = cut(tile, pos, slot)

    def times(slot, layer, re, im):
        t_re, t_im = window[slot, 0, layer], window[slot, 1, layer]
        return re * t_re - im * t_im, re * t_im + im * t_re

    def times_conj(slot, layer, re, im):
        t_re, t_im = window[slot, 0, layer], window[slot, 1, layer]
        return re * t_re + im * t_im, im * t_re - re * t_im

    def store_term(slot, layer, re, im):
        p_re, p_im = waves[slot, layer, 0], waves[slot, layer, 1]
        term_re = p_re * re + p_im * im
        term_im = p_re * im - p_im * re
        top[slot, 0, layer] = term_re[:HALF]
        top[slot, 1, layer] = term_im[:HALF]
        bottom[slot, 0, layer] = term_re[HALF:]
        bottom[slot, 1, layer] = term_im[HALF:]

    def send_terms(slot):
        for side, there, device in sides:
            @pl.when(there)
            def _():
                grad_copy(side, slot, device).start()

        own_copy(slot).start()

    for load in tables_in:
        load.wait()

    @pl.when(core == 0)
    def _():
        def forward(slot):
            build_window(slot)
            row = pos[0, slot] - lat * HALF
            _, lane = column_block(pos, slot)
            re = pltpu.roll(pltpu.roll(probe[0], row, 0), lane, 1)
            im = pltpu.roll(pltpu.roll(probe[1], row, 0), lane, 1)
            waves[slot, 0, 0] = re
            waves[slot, 0, 1] = im
            re, im = product(mats, PROP, *times(slot, 0, re, im))
            waves[slot, 1, 0] = re
            waves[slot, 1, 1] = im
            re, im = product(mats, PROP, *times(slot, 1, re, im))
            wave_out[slot, 0] = re
            wave_out[slot, 1] = im
            wave_copy(slot).start()

        def backward(slot):
            wave_copy(slot).wait_recv()
            re, im = product(mats, PROP_CONJ, wave_in[slot, 0], wave_in[slot, 1])
            store_term(slot, 1, re, im)
            re, im = product(mats, PROP_CONJ, *times_conj(slot, 1, re, im))
            store_term(slot, 0, re, im)
            send_terms(slot)

        def step(at, carry):
            @pl.when(at < slots)
            def _():
                forward(at)

            @pl.when(at >= 2)
            def _():
                backward(at - 2)

            return carry

        lax.fori_loop(0, slots + 2, step, 0)

    @pl.when(core == 1)
    def _():
        def whole(slot, carry):
            build_window(slot)
            wave_copy(slot).wait_recv()
            re, im = wave_in[slot, 0], wave_in[slot, 1]
            waves[slot, 0, 0] = re
            waves[slot, 0, 1] = im
            re, im = product(mats, PROP, *times(slot, 0, re, im))
            waves[slot, 1, 0] = re
            waves[slot, 1, 1] = im
            re, im = product(mats, DFT, *times(slot, 1, re, im))
            live = jnp.where(slot < counts[0], 1.0, 0.0).astype(jnp.float32)
            weight = live * (1.0 - amp[slot] / jnp.sqrt(re * re + im * im + 1.0))
            re, im = product(mats, DFT_CONJ, weight * re, weight * im)
            store_term(slot, 1, re, im)
            re, im = product(mats, PROP_CONJ, *times_conj(slot, 1, re, im))
            store_term(slot, 0, re, im)
            re, im = times_conj(slot, 0, re, im)
            wave_out[slot, 0] = re
            wave_out[slot, 1] = im
            wave_copy(slot).start()
            send_terms(slot)
            return carry

        lax.fori_loop(0, slots, whole, 0)

    for k in range(slots):
        for part in range(2):
            pos_out[0, part, k] = pos[part, k]
            pos_out[1, part, k] = pos_prev[part, k]
            pos_out[2, part, k] = pos_next[part, k]

    def finish(slot, carry):
        own_copy(slot).wait()
        wave_copy(slot).wait_send()
        for side, there, device in sides:
            @pl.when(there)
            def _():
                win_copy(side, slot, device).wait_send()
                grad_copy(side, slot, device).wait_send()
                grad_arrival(side, slot, device).wait_recv()

        return carry

    for side, there, device in sides:
        @pl.when(there)
        def _():
            pos_copy(side, device).wait_send()

    lax.fori_loop(0, slots, finish, 0)


def place_kernel(n, places, own, from_prev, from_next, out, sums):
    lat = lax.axis_index("lat")
    blocks = sums.shape[0] - 2
    pos, pos_prev, pos_next = places.at[0], places.at[1], places.at[2]
    sums[...] = jnp.zeros_like(sums)
    shape = (2, 2, HALF, WIN)
    rows = lax.broadcasted_iota(jnp.int32, shape, 2)
    lanes = lax.broadcasted_iota(jnp.int32, shape, 3)

    def add(where, slot, piece, keep):
        block, lane = column_block(where, slot)
        if keep is not None:
            piece = jnp.where(keep, piece, 0.0)
        sums[block] += jnp.where(lanes >= lane, piece, 0.0)
        sums[block + 1] += jnp.where(lanes >= lane, 0.0, piece)

    def one(slot, carry):
        add(pos, slot, own[slot], None)

        @pl.when(lat > 0)
        def _():
            row = pos_prev[0, slot] - (lat - 1) * HALF
            add(pos_prev, slot, from_prev[slot], rows < row)

        @pl.when(lat < n - 1)
        def _():
            row = pos_next[0, slot] - (lat + 1) * HALF
            add(pos_next, slot, from_next[slot], rows >= row)

        return carry

    lax.fori_loop(0, pos.shape[1], one, 0)
    for k in range(blocks):
        out[:, :, :, k * WIN : (k + 1) * WIN] = sums[k + 1]


def on_device(n, trans, probe, amp, pos, counts):
    slots = pos.shape[0]
    pos = pos.T
    blocks = trans.shape[3] // WIN
    smem = pl.BlockSpec(memory_space=pltpu.SMEM)
    vmem = pl.BlockSpec(memory_space=pltpu.VMEM)
    hbm = pl.BlockSpec(memory_space=pltpu.HBM)
    piece = (slots, 2, 2, HALF, WIN)
    wave = (slots, 2, WIN, WIN)
    f32 = jnp.float32
    mats = jnp.asarray(tables())
    held = [pltpu.with_memory_space_constraint(x, pltpu.HBM) for x in (pos, trans, probe, amp, mats)]
    from_prev, from_next, own, places = pl.pallas_call(
        functools.partial(kernel, n),
        out_shape=[pltpu.VMEM(piece, f32)] * 3 + [jax.ShapeDtypeStruct((3, *pos.shape), jnp.int32)],
        in_specs=[hbm] * 6,
        out_specs=[vmem, vmem, vmem, smem],
        scratch_shapes=[
            pltpu.VMEM((blocks + 2, 2, 2, HALF, WIN), f32),
            pltpu.VMEM(probe.shape, f32),
            pltpu.VMEM(amp.shape, f32),
            pltpu.VMEM(mats.shape, jnp.bfloat16),
            pltpu.VMEM(piece, f32),
            pltpu.VMEM(piece, f32),
            pltpu.VMEM(piece, f32),
            pltpu.VMEM(piece, f32),
            pltpu.VMEM((slots, 2, 2, WIN, WIN), f32),
            pltpu.VMEM((slots, 2, 2, WIN, WIN), f32),
            pltpu.VMEM(wave, f32),
            pltpu.VMEM(wave, f32),
            pltpu.VMEM(piece, f32),
            pltpu.VMEM(piece, f32),
            pltpu.SMEM(pos.shape, jnp.int32),
            pltpu.SMEM(counts.shape, jnp.int32),
            pltpu.SMEM(pos.shape, jnp.int32),
            pltpu.SMEM(pos.shape, jnp.int32),
            pltpu.SemaphoreType.DMA((blocks,)),
            pltpu.SemaphoreType.DMA((3,)),
            pltpu.SemaphoreType.DMA((2,)),
            pltpu.SemaphoreType.DMA((2,)),
            pltpu.SemaphoreType.DMA((2,)),
            pltpu.SemaphoreType.DMA((2, slots)),
            pltpu.SemaphoreType.DMA((2, slots)),
            pltpu.SemaphoreType.DMA((slots,)),
            pltpu.SemaphoreType.DMA((slots,)),
            pltpu.SemaphoreType.DMA((2, slots)),
            pltpu.SemaphoreType.DMA((2, slots)),
            pltpu.SemaphoreType.DMA((slots,)),
        ],
        compiler_params=pltpu.CompilerParams(
            collective_id=0, has_side_effects=True, vmem_limit_bytes=40 << 20
        ),
        name="windows",
    )(held[0], counts, *held[1:])
    return pl.pallas_call(
        functools.partial(place_kernel, n),
        out_shape=jax.ShapeDtypeStruct(trans.shape, f32),
        in_specs=[smem, vmem, vmem, vmem],
        out_specs=vmem,
        scratch_shapes=[pltpu.VMEM((blocks + 2, 2, 2, HALF, WIN), f32)],
        compiler_params=pltpu.CompilerParams(vmem_limit_bytes=40 << 20),
        name="place",
    )(places, own, from_prev, from_next)


def solution(mesh):
    placed = (P(None, "depth", "lat", None), P(), P("lat", None, None), P("lat", None), P("lat"))
    return jax.shard_map(
        functools.partial(on_device, mesh.shape["lat"]),
        mesh=mesh,
        in_specs=placed,
        out_specs=P(None, "depth", "lat", None),
        check_vma=False,
    )
```

```python
import functools

import jax
import jax.numpy as jnp
import ml_dtypes
import numpy as np
from jax import lax
from jax.experimental import pallas as pl
from jax.experimental.pallas import tpu as pltpu
from jax.sharding import PartitionSpec as P

PROP_COEF = 40.0
WIN = 128
HALF = 64
EARLY = 8
MESH = pl.DeviceIdType.MESH
PROP, PROP_CONJ, DFT, DFT_CONJ = range(4)


def tables():
    index = np.arange(WIN)
    dft = np.exp(-2j * np.pi * (np.outer(index, index) % WIN) / WIN) / np.sqrt(WIN)
    freq = ((index + WIN // 2) % WIN - WIN // 2) / WIN
    prop = dft.conj() @ np.diag(np.exp(-1j * PROP_COEF * freq * freq)) @ dft
    terms = []
    for matrix in (prop, prop.conj(), dft, dft.conj()):
        real = np.block([[matrix.real, -matrix.imag], [matrix.imag, matrix.real]])
        high = real.astype(ml_dtypes.bfloat16)
        low = (real - high.astype(np.float64)).astype(ml_dtypes.bfloat16)
        terms.append(np.stack([high, low]))
    return np.stack(terms)


def split(values):
    high = values.astype(jnp.bfloat16)
    low = (values - high.astype(jnp.float32)).astype(jnp.bfloat16)
    return high, low


def product(mats, which, re, im):
    conj = which ^ 1
    high, low = split(jnp.concatenate([re, im], axis=1))
    right = jnp.concatenate([mats[conj, 0], mats[conj, 0], mats[conj, 1]], axis=0)
    first = jnp.dot(
        jnp.concatenate([high, low, high], axis=1), right, preferred_element_type=jnp.float32
    )
    high, low = split(first)
    left = jnp.concatenate(
        [mats[which, 0, :, :WIN], mats[which, 0, :, :WIN], mats[which, 1, :, :WIN]], axis=1
    )
    second = jnp.dot(
        left, jnp.concatenate([high, low, high], axis=0), preferred_element_type=jnp.float32
    )
    return second[:WIN, :WIN] - second[WIN:, WIN:], second[:WIN, WIN:] + second[WIN:, :WIN]


def column_block(pos, slot):
    column = pos[1, slot] + HALF
    return lax.shift_right_logical(column, 7), column & (WIN - 1)


def cut(tile, pos, slot, rows):
    block, lane = column_block(pos, slot)
    first, second = tile[block, :, :, rows], tile[block + 1, :, :, rows]
    lanes = lax.broadcasted_iota(jnp.int32, first.shape, 3)
    return jnp.where(lanes >= lane, first, second)


ALL = slice(0, HALF)
FIRST = slice(0, EARLY)
REST = slice(EARLY, HALF)


def kernel(
    n, pos_hbm, counts_hbm, trans, probe_hbm, amp_hbm, mats_hbm,
    grad,
    tile, probe, amp, mats, full_prev, full_next, to_prev, to_next, to_partner, early_prev, early_next,
    have_prev, have_next, have_own, from_prev, from_next, own, window, waves, top, bottom, pos, counts, pos_prev, pos_next,
    tile_sem, table_sem, pos_sem, pos_send, pos_recv, full_send, full_recv, early_send, early_recv,
    part_send, part_recv, win_send, win_recv, grad_send, grad_recv, bottom_send, bottom_recv,
):
    core = lax.axis_index("depth")
    lat = lax.axis_index("lat")
    has_prev = lat > 0
    has_next = lat < n - 1
    slots = pos.shape[1]
    turns = slots // 2
    blocks = tile.shape[0] - 2
    partner = (1 - core, lat)
    sides = (
        (0, has_prev, lat - 1, pos_prev, full_prev, have_prev, from_prev),
        (1, has_next, lat + 1, pos_next, full_next, have_next, from_next),
    )

    scalars = [
        pltpu.make_async_copy(source, target, pos_sem.at[k])
        for k, (source, target) in enumerate(((pos_hbm, pos), (counts_hbm, counts)))
    ]
    loads = [
        pltpu.make_async_copy(
            trans.at[:, :, :, pl.ds(k * WIN, WIN)], tile.at[k + 1], tile_sem.at[k]
        )
        for k in range(blocks)
    ]
    tables_in = [
        pltpu.make_async_copy(source, target, table_sem.at[k])
        for k, (source, target) in enumerate(((mats_hbm, mats), (probe_hbm, probe), (amp_hbm, amp)))
    ]
    for load in scalars + loads + tables_in:
        load.start()

    barrier = pltpu.get_barrier_semaphore()
    for _, there, place, *_rest in sides:
        @pl.when(there)
        def _():
            for k in (core, 1 - core):
                pl.semaphore_signal(barrier, inc=1, device_id=(k, place), device_id_type=MESH)

    pl.semaphore_signal(barrier, inc=1, device_id=partner, device_id_type=MESH)

    grad[...] = jnp.zeros_like(grad)
    for padded in (tile, full_prev, full_next):
        padded[0] = jnp.zeros(padded.shape[1:], jnp.float32)
        padded[blocks + 1] = jnp.zeros(padded.shape[1:], jnp.float32)
    for _, there, _place, where, full, have, _arrived in sides:
        @pl.when(jnp.logical_not(there))
        def _():
            have[...] = jnp.zeros_like(have)
            for k in range(slots):
                where[0, k] = 0
                where[1, k] = 0

    for load in scalars:
        load.wait()
    pl.semaphore_wait(
        barrier, 1 + 2 * has_prev.astype(jnp.int32) + 2 * has_next.astype(jnp.int32)
    )

    def remote(source, target, send, recv, device):
        return pltpu.make_async_remote_copy(
            src_ref=source, dst_ref=target, send_sem=send, recv_sem=recv,
            device_id=device, device_id_type=MESH,
        )

    def pos_copy(side, place):
        return remote(pos, sides[1 - side][3], pos_send.at[side], pos_recv.at[1 - side], (core, place))

    def pos_arrival(side, place):
        return remote(pos, sides[side][3], pos_send.at[side], pos_recv.at[side], (core, place))

    def full_copy(side, place):
        return remote(
            tile.at[pl.ds(1, blocks), :, :, pl.ds(0, EARLY)], sides[1 - side][4].at[pl.ds(1, blocks)],
            full_send.at[side], full_recv.at[1 - side], (core, place),
        )

    def full_arrival(side, place):
        return remote(
            tile.at[pl.ds(1, blocks), :, :, pl.ds(0, EARLY)], sides[side][4].at[pl.ds(1, blocks)],
            full_send.at[side], full_recv.at[side], (core, place),
        )

    def win_copy(side, turn, to, place):
        slot = 2 * turn + to
        return remote(
            (to_prev, to_next)[side].at[slot], sides[1 - side][5].at[turn, core, :, :, pl.ds(EARLY, HALF - EARLY)],
            win_send.at[side, slot], win_recv.at[1 - side, turn, core], (to, place),
        )

    def win_arrival(side, turn, group, place):
        return remote(
            to_prev.at[0], sides[side][5].at[turn, group, :, :, pl.ds(EARLY, HALF - EARLY)],
            win_send.at[side, 0], win_recv.at[side, turn, group], (core, place),
        )

    def early_copy(side, turn, group):
        return remote(
            (early_prev, early_next)[side].at[turn], sides[side][5].at[turn, group, :, :, pl.ds(0, EARLY)],
            early_send.at[side, turn], early_recv.at[side, turn], partner,
        )

    def part_copy(turn, group):
        return remote(
            to_partner.at[turn], have_own.at[turn, group], part_send.at[turn], part_recv.at[turn], partner
        )

    def grad_copy(side, turn, layer, to, place):
        slot = 2 * turn + core
        return remote(
            top.at[turn, layer], sides[1 - side][6].at[slot, layer % 2],
            grad_send.at[side, turn, layer], grad_recv.at[1 - side, slot, layer % 2], (to, place),
        )

    def grad_arrival(side, slot, part, place):
        return remote(
            top.at[0, 0], sides[side][6].at[slot, part],
            grad_send.at[side, 0, 0], grad_recv.at[side, slot, part], (core, place),
        )

    def bottom_copy(turn, part, slot):
        return remote(
            bottom.at[turn, part], own.at[slot, part], bottom_send.at[turn, part], bottom_recv.at[turn, part], partner
        )

    for side, there, place, *_rest in sides:
        @pl.when(there)
        def _():
            pos_copy(side, place).start()

    for load in loads:
        load.wait()
    for side, there, place, *_rest in sides:
        @pl.when(there)
        def _():
            full_copy(side, place).start()

    def own_windows(turn, carry):
        have_own[turn, core] = cut(tile, pos, 2 * turn + core, ALL)
        to_partner[turn] = cut(tile, pos, 2 * turn + 1 - core, ALL)
        part_copy(turn, core).start()
        return carry

    lax.fori_loop(0, turns, own_windows, 0)

    for side, there, place, *_rest in sides:
        @pl.when(there)
        def _():
            pos_arrival(side, place).wait_recv()

    def send_windows(turn, carry):
        for to in (core, 1 - core):
            slot = 2 * turn + to
            for side, there, place, where, *_rest in sides:
                @pl.when(there)
                def _():
                    (to_prev, to_next)[side][slot] = cut(tile, where, slot, REST)
                    win_copy(side, turn, to, place).start()

        return carry

    lax.fori_loop(0, turns, send_windows, 0)

    def early_windows(turn, carry):
        for side, there, place, _where, full, have, _arrived in sides:
            @pl.when(there)
            def _():
                have[turn, core, :, :, FIRST] = cut(full, pos, 2 * turn + core, FIRST)
                (early_prev, early_next)[side][turn] = cut(full, pos, 2 * turn + 1 - core, FIRST)
                early_copy(side, turn, core).start()

        return carry

    for side, there, place, *_rest in sides:
        @pl.when(there)
        def _():
            full_arrival(side, place).wait_recv()

    lax.fori_loop(0, turns, early_windows, 0)

    for load in tables_in:
        load.wait()

    def build_window(turn, group):
        for side, there, place, *_rest in sides:
            @pl.when(there)
            def _():
                win_arrival(side, turn, group, place).wait_recv()

        @pl.when(core != group)
        def _():
            part_copy(turn, group).wait_recv()
            for side, there, place, *_rest in sides:
                @pl.when(there)
                def _():
                    early_copy(side, turn, group).wait_recv()

        row = pos[0, 2 * turn + core] - lat * HALF
        rows = lax.broadcasted_iota(jnp.int32, (2, 2, HALF, WIN), 2)
        window[group, :, :, :HALF] = jnp.where(rows >= row, have_prev[turn, group], have_next[turn, group])
        window[group, :, :, HALF:] = have_own[turn, group]

    def times(layer, re, im):
        t_re, t_im = window[layer // 2, 0, layer % 2], window[layer // 2, 1, layer % 2]
        return re * t_re - im * t_im, re * t_im + im * t_re

    def times_conj(layer, re, im):
        t_re, t_im = window[layer // 2, 0, layer % 2], window[layer // 2, 1, layer % 2]
        return re * t_re + im * t_im, im * t_re - re * t_im

    def send_term(turn, layer, re, im):
        p_re, p_im = waves[layer, 0], waves[layer, 1]
        term_re = p_re * re + p_im * im
        term_im = p_re * im - p_im * re
        top[turn, layer, 0] = term_re[:HALF]
        top[turn, layer, 1] = term_im[:HALF]
        slot = 2 * turn + core
        group, part = layer // 2, layer % 2
        for at_home, to in ((core == group, core), (core != group, 1 - core)):
            for side, there, place, *_rest in sides:
                @pl.when(jnp.logical_and(there, at_home))
                def _():
                    grad_copy(side, turn, layer, to, place).start()

        @pl.when(core == group)
        def _():
            own[slot, part, 0] = term_re[HALF:]
            own[slot, part, 1] = term_im[HALF:]

        @pl.when(core != group)
        def _():
            bottom[turn, part, 0] = term_re[HALF:]
            bottom[turn, part, 1] = term_im[HALF:]
            bottom_copy(turn, part, slot).start()

    def whole(turn, carry):
        slot = 2 * turn + core
        row = pos[0, slot] - lat * HALF
        _, lane = column_block(pos, slot)
        re = pltpu.roll(pltpu.roll(probe[0], row, 0), lane, 1)
        im = pltpu.roll(pltpu.roll(probe[1], row, 0), lane, 1)
        for layer in range(4):
            if layer % 2 == 0:
                build_window(turn, layer // 2)
            waves[layer, 0] = re
            waves[layer, 1] = im
            re, im = product(mats, PROP if layer < 3 else DFT, *times(layer, re, im))
        live = jnp.where(slot < counts[0], 1.0, 0.0).astype(jnp.float32)
        weight = live * (1.0 - amp[slot] / jnp.sqrt(re * re + im * im + 1.0))
        re, im = product(mats, DFT_CONJ, weight * re, weight * im)
        for layer in range(3, -1, -1):
            send_term(turn, layer, re, im)
            if layer > 0:
                re, im = product(mats, PROP_CONJ, *times_conj(layer, re, im))
        return carry

    lax.fori_loop(0, turns, whole, 0)

    rows = lax.broadcasted_iota(jnp.int32, (2, HALF, WIN), 1)
    lanes = lax.broadcasted_iota(jnp.int32, (2, HALF, WIN), 2)

    def add(where, slot, part, piece):
        begin = where[1, slot] - HALF
        for k in range(blocks):
            offset = lanes + (k * WIN - begin)
            inside = jnp.logical_and(offset >= 0, offset < WIN)
            grad[:, part, :, k * WIN : (k + 1) * WIN] += jnp.where(inside, piece, 0.0)

    def add_own(turn, carry):
        for k in range(2):
            slot = 2 * turn + k
            for part in range(2):
                @pl.when(core != k)
                def _():
                    bottom_copy(turn, part, slot).wait_recv()

                add(pos, slot, part, own[slot, part])
        return carry

    def add_others(slot, carry):
        for part in (1, 0):
            for side, there, place, where, _full, _have, arrived in sides:
                @pl.when(there)
                def _():
                    grad_arrival(side, slot, part, place).wait_recv()
                    row = where[0, slot] - place * HALF
                    keep = rows < row if side == 0 else rows >= row
                    add(where, slot, part, jnp.where(keep, arrived[slot, part], 0.0))

        return carry

    lax.fori_loop(0, turns, add_own, 0)
    lax.fori_loop(0, slots, add_others, 0)

    for side, there, place, *_rest in sides:
        @pl.when(there)
        def _():
            pos_copy(side, place).wait_send()
            full_copy(side, place).wait_send()

    def finish(turn, carry):
        part_copy(turn, core).wait_send()
        for part in range(2):
            bottom_copy(turn, part, 2 * turn + 1 - core).wait_send()
        for side, there, place, *_rest in sides:
            @pl.when(there)
            def _():
                early_copy(side, turn, core).wait_send()
                for layer in range(4):
                    grad_copy(side, turn, layer, core, place).wait_send()
                for to in (core, 1 - core):
                    win_copy(side, turn, to, place).wait_send()

        return carry

    lax.fori_loop(0, turns, finish, 0)


def on_device(n, trans, probe, amp, pos, counts):
    slots = pos.shape[0]
    turns = slots // 2
    pos = pos.T
    blocks = trans.shape[3] // WIN
    vmem = pl.BlockSpec(memory_space=pltpu.VMEM)
    hbm = pl.BlockSpec(memory_space=pltpu.HBM)
    f32 = jnp.float32
    piece = (slots, 2, 2, HALF, WIN)
    mats = jnp.asarray(tables())
    held = [pltpu.with_memory_space_constraint(x, pltpu.HBM) for x in (pos, trans, probe, amp, mats)]
    sem = pltpu.SemaphoreType.DMA
    return pl.pallas_call(
        functools.partial(kernel, n),
        out_shape=pltpu.VMEM(trans.shape, f32),
        in_specs=[hbm] * 6,
        out_specs=vmem,
        scratch_shapes=[
            pltpu.VMEM((blocks + 2, 2, 2, HALF, WIN), f32),
            pltpu.VMEM(probe.shape, f32),
            pltpu.VMEM(amp.shape, f32),
            pltpu.VMEM(mats.shape, jnp.bfloat16),
            pltpu.VMEM((blocks + 2, 2, 2, EARLY, WIN), f32),
            pltpu.VMEM((blocks + 2, 2, 2, EARLY, WIN), f32),
            pltpu.VMEM((slots, 2, 2, HALF - EARLY, WIN), f32),
            pltpu.VMEM((slots, 2, 2, HALF - EARLY, WIN), f32),
            pltpu.VMEM((turns, 2, 2, HALF, WIN), f32),
            pltpu.VMEM((turns, 2, 2, EARLY, WIN), f32),
            pltpu.VMEM((turns, 2, 2, EARLY, WIN), f32),
            pltpu.VMEM((turns, 2, 2, 2, HALF, WIN), f32),
            pltpu.VMEM((turns, 2, 2, 2, HALF, WIN), f32),
            pltpu.VMEM((turns, 2, 2, 2, HALF, WIN), f32),
            pltpu.VMEM(piece, f32),
            pltpu.VMEM(piece, f32),
            pltpu.VMEM(piece, f32),
            pltpu.VMEM((2, 2, 2, WIN, WIN), f32),
            pltpu.VMEM((4, 2, WIN, WIN), f32),
            pltpu.VMEM((turns, 4, 2, HALF, WIN), f32),
            pltpu.VMEM((turns, 2, 2, HALF, WIN), f32),
            pltpu.SMEM(pos.shape, jnp.int32),
            pltpu.SMEM(counts.shape, jnp.int32),
            pltpu.SMEM(pos.shape, jnp.int32),
            pltpu.SMEM(pos.shape, jnp.int32),
            sem((blocks,)),
            sem((3,)),
            sem((2,)),
            sem((2,)),
            sem((2,)),
            sem((2,)),
            sem((2,)),
            sem((2, turns)),
            sem((2, turns)),
            sem((turns,)),
            sem((turns,)),
            sem((2, slots)),
            sem((2, turns, 2)),
            sem((2, turns, 4)),
            sem((2, slots, 2)),
            sem((turns, 2)),
            sem((turns, 2)),
        ],
        compiler_params=pltpu.CompilerParams(
            collective_id=0, has_side_effects=True, vmem_limit_bytes=40 << 20
        ),
        name="windows",
    )(held[0], counts, *held[1:])


def solution(mesh):
    placed = (P(None, "depth", "lat", None), P(), P("lat", None, None), P("lat", None), P("lat"))
    return jax.shard_map(
        functools.partial(on_device, mesh.shape["lat"]),
        mesh=mesh,
        in_specs=placed,
        out_specs=P(None, "depth", "lat", None),
        check_vma=False,
    )
```

```python
import functools

import jax
import jax.numpy as jnp
import ml_dtypes
import numpy as np
from jax import lax
from jax.experimental import pallas as pl
from jax.experimental.pallas import tpu as pltpu
from jax.sharding import PartitionSpec as P

PROP_COEF = 40.0
WIN = 128
HALF = 64
EARLY = 8
PLANE = 16
DETOUR = 3
MESH = pl.DeviceIdType.MESH
PROP, PROP_CONJ, DFT, DFT_CONJ = range(4)


def tables():
    index = np.arange(WIN)
    dft = np.exp(-2j * np.pi * (np.outer(index, index) % WIN) / WIN) / np.sqrt(WIN)
    freq = ((index + WIN // 2) % WIN - WIN // 2) / WIN
    prop = dft.conj() @ np.diag(np.exp(-1j * PROP_COEF * freq * freq)) @ dft
    terms = []
    for matrix in (prop, prop.conj(), dft, dft.conj()):
        real = np.block([[matrix.real, -matrix.imag], [matrix.imag, matrix.real]])
        high = real.astype(ml_dtypes.bfloat16)
        low = (real - high.astype(np.float64)).astype(ml_dtypes.bfloat16)
        terms.append(np.stack([high, low]))
    return np.stack(terms)


def split(values):
    high = values.astype(jnp.bfloat16)
    low = (values - high.astype(jnp.float32)).astype(jnp.bfloat16)
    return high, low


def product(mats, which, re, im):
    conj = which ^ 1
    high, low = split(jnp.concatenate([re, im], axis=1))
    right = jnp.concatenate([mats[conj, 0], mats[conj, 0], mats[conj, 1]], axis=0)
    first = jnp.dot(
        jnp.concatenate([high, low, high], axis=1), right, preferred_element_type=jnp.float32
    )
    high, low = split(first)
    left = jnp.concatenate(
        [mats[which, 0, :, :WIN], mats[which, 0, :, :WIN], mats[which, 1, :, :WIN]], axis=1
    )
    second = jnp.dot(
        left, jnp.concatenate([high, low, high], axis=0), preferred_element_type=jnp.float32
    )
    return second[:WIN, :WIN] - second[WIN:, WIN:], second[:WIN, WIN:] + second[WIN:, :WIN]


def column_block(pos, slot):
    column = pos[1, slot] + HALF
    return lax.shift_right_logical(column, 7), column & (WIN - 1)


def cut(tile, pos, slot, rows):
    block, lane = column_block(pos, slot)
    first, second = tile[block, :, :, rows], tile[block + 1, :, :, rows]
    lanes = lax.broadcasted_iota(jnp.int32, first.shape, 3)
    return jnp.where(lanes >= lane, first, second)


DETOURED = (3, 2)
ALL = slice(0, HALF)
FIRST = slice(0, EARLY)
SECOND = slice(EARLY, 2 * EARLY)
REST = slice(EARLY, HALF)


def kernel(
    n, pos_hbm, counts_hbm, trans, probe_hbm, amp_hbm, mats_hbm,
    grad,
    tile, probe, amp, mats, full_prev, full_next, more_prev, to_prev, to_next, to_partner, early_prev, early_next, early_more,
    have_prev, have_next, have_own, from_prev, from_next, own, window, waves, top, bottom, passed, pos, counts, pos_prev, pos_next, pos_pass,
    here_sem, tile_sem, table_sem, pos_sem, pos_send, pos_recv, full_send, full_recv, early_send, early_recv,
    more_send, more_recv, extra_send, extra_recv,
    part_send, part_recv, win_send, win_recv, grad_send, grad_recv, bottom_send, bottom_recv, passed_send, passed_recv, pass_send, pass_recv,
):
    core = lax.axis_index("depth")
    lat = lax.axis_index("lat")
    has_prev = lat > 0
    has_next = lat < n - 1
    far_prev = jnp.logical_and(has_prev, lax.rem(lat, PLANE) == 0)
    far_next = jnp.logical_and(has_next, lax.rem(lat, PLANE) == PLANE - 1)
    first_of_plane, last_of_plane = lat - DETOUR, lat + DETOUR
    passes_up = jnp.logical_and(first_of_plane > 0, lax.rem(first_of_plane, PLANE) == 0)
    passes_down = jnp.logical_and(last_of_plane < n - 1, lax.rem(last_of_plane, PLANE) == PLANE - 1)
    passes = jnp.logical_or(passes_up, passes_down)
    slots = pos.shape[1]
    turns = slots // 2
    blocks = tile.shape[0] - 2
    partner = (1 - core, lat)
    sides = (
        (0, has_prev, lat - 1, pos_prev, full_prev, have_prev, from_prev),
        (1, has_next, lat + 1, pos_next, full_next, have_next, from_next),
    )

    scalars = [
        pltpu.make_async_copy(source, target, pos_sem.at[k])
        for k, (source, target) in enumerate(((pos_hbm, pos), (counts_hbm, counts)))
    ]
    loads = [
        pltpu.make_async_copy(
            trans.at[:, :, :, pl.ds(k * WIN, WIN)], tile.at[k + 1], tile_sem.at[k]
        )
        for k in range(blocks)
    ]
    tables_in = [
        pltpu.make_async_copy(source, target, table_sem.at[k])
        for k, (source, target) in enumerate(((mats_hbm, mats), (probe_hbm, probe), (amp_hbm, amp)))
    ]
    for load in scalars + loads + tables_in:
        load.start()

    barrier = pltpu.get_barrier_semaphore()
    near_prev = jnp.logical_and(has_prev, jnp.logical_not(far_prev))
    near_next = jnp.logical_and(has_next, jnp.logical_not(far_next))
    first, second = core == 0, core == 1
    to_same = ((has_prev, lat - 1), (jnp.logical_or(near_next, jnp.logical_and(far_next, first)), lat + 1))
    to_other = ((has_prev, lat - 1), (jnp.logical_or(near_next, jnp.logical_and(far_next, second)), lat + 1))
    for targets, k in ((to_same, core), (to_other, 1 - core)):
        for there, place in targets:
            @pl.when(there)
            def _():
                pl.semaphore_signal(barrier, inc=1, device_id=(k, place), device_id_type=MESH)

    pl.semaphore_signal(barrier, inc=1, device_id=partner, device_id_type=MESH)

    @pl.when(passes_up)
    def _():
        pl.semaphore_signal(barrier, inc=1, device_id=(core, lat - DETOUR - 1), device_id_type=MESH)

    @pl.when(passes_down)
    def _():
        pl.semaphore_signal(barrier, inc=1, device_id=(core, lat + DETOUR + 1), device_id_type=MESH)

    @pl.when(jnp.logical_and(far_next, first))
    def _():
        pl.semaphore_signal(barrier, inc=1, device_id=(1 - core, lat - DETOUR), device_id_type=MESH)

    for flag, place in ((far_prev, lat + DETOUR), (far_next, lat - DETOUR)):
        @pl.when(jnp.logical_and(flag, core == 1))
        def _():
            for k in (core, 1 - core):
                pl.semaphore_signal(barrier, inc=1, device_id=(k, place), device_id_type=MESH)

    grad[...] = jnp.zeros_like(grad)
    for padded in (tile, full_prev, full_next, more_prev):
        padded[0] = jnp.zeros(padded.shape[1:], jnp.float32)
        padded[blocks + 1] = jnp.zeros(padded.shape[1:], jnp.float32)
    for _, there, _place, where, full, have, _arrived in sides:
        @pl.when(jnp.logical_not(there))
        def _():
            have[...] = jnp.zeros_like(have)
            for k in range(slots):
                where[0, k] = 0
                where[1, k] = 0

    for load in scalars:
        load.wait()
    pl.semaphore_wait(
        barrier,
        1 + 2 * jnp.logical_or(near_prev, jnp.logical_and(far_prev, first)).astype(jnp.int32)
        + 2 * has_next.astype(jnp.int32) + jnp.logical_and(passes_down, second).astype(jnp.int32)
        + far_prev.astype(jnp.int32) + far_next.astype(jnp.int32) + passes.astype(jnp.int32),
    )

    def remote(source, target, send, recv, device):
        return pltpu.make_async_remote_copy(
            src_ref=source, dst_ref=target, send_sem=send, recv_sem=recv,
            device_id=device, device_id_type=MESH,
        )

    def pos_copy(side, place):
        return remote(pos, sides[1 - side][3], pos_send.at[side], pos_recv.at[1 - side], (core, place))

    def pos_arrival(side, place):
        return remote(pos, sides[side][3], pos_send.at[side], pos_recv.at[side], (core, place))

    def full_copy(side, place):
        return remote(
            tile.at[pl.ds(1, blocks), :, :, pl.ds(0, EARLY)], sides[1 - side][4].at[pl.ds(1, blocks)],
            full_send.at[side], full_recv.at[1 - side], (core, place),
        )

    def full_arrival(side, place):
        return remote(
            tile.at[pl.ds(1, blocks), :, :, pl.ds(0, EARLY)], sides[side][4].at[pl.ds(1, blocks)],
            full_send.at[side], full_recv.at[side], (core, place),
        )

    def more_copy():
        return remote(
            tile.at[pl.ds(1, blocks), :, :, pl.ds(EARLY, EARLY)], more_prev.at[pl.ds(1, blocks)],
            more_send, more_recv, (core, lat + 1),
        )

    def more_arrival():
        return remote(
            tile.at[pl.ds(1, blocks), :, :, pl.ds(EARLY, EARLY)], more_prev.at[pl.ds(1, blocks)],
            more_send, more_recv, (core, lat - 1),
        )

    def when_near_or_far(side, there, far, act):
        if side == 0:
            pl.when(there)(functools.partial(act, EARLY))
        else:
            pl.when(jnp.logical_and(there, jnp.logical_not(far)))(functools.partial(act, EARLY))
            pl.when(jnp.logical_and(there, far))(functools.partial(act, 2 * EARLY))

    def win_copy(side, turn, to, place, begin):
        slot, rows = 2 * turn + to, HALF - begin
        return remote(
            (to_prev, to_next)[side].at[slot, :, :, pl.ds(begin - EARLY, rows)],
            sides[1 - side][5].at[turn, core, :, :, pl.ds(begin, rows)],
            win_send.at[side, slot], win_recv.at[1 - side, turn, core], (to, place),
        )

    def win_arrival(side, turn, group, place, begin):
        rows = HALF - begin
        return remote(
            to_prev.at[0, :, :, pl.ds(begin - EARLY, rows)], sides[side][5].at[turn, group, :, :, pl.ds(begin, rows)],
            win_send.at[side, 0], win_recv.at[side, turn, group], (core, place),
        )

    def extra_copy(turn, group):
        return remote(
            early_more.at[turn], have_prev.at[turn, group, :, :, pl.ds(EARLY, EARLY)],
            extra_send.at[turn], extra_recv.at[turn], partner,
        )

    def early_copy(side, turn, group):
        return remote(
            (early_prev, early_next)[side].at[turn], sides[side][5].at[turn, group, :, :, pl.ds(0, EARLY)],
            early_send.at[side, turn], early_recv.at[side, turn], partner,
        )

    def part_copy(turn, group):
        return remote(
            to_partner.at[turn], have_own.at[turn, group], part_send.at[turn], part_recv.at[turn], partner
        )

    def grad_copy(side, turn, layer, to, place):
        slot = 2 * turn + core
        return remote(
            top.at[turn, layer], sides[1 - side][6].at[slot, layer % 2],
            grad_send.at[side, turn, layer], grad_recv.at[1 - side, slot, layer % 2], (to, place),
        )

    def grad_arrival(side, slot, part, place):
        return remote(
            top.at[0, 0], sides[side][6].at[slot, part],
            grad_send.at[side, 0, 0], grad_recv.at[side, slot, part], (core, place),
        )

    def detour_copy(side, turn, layer):
        return remote(
            top.at[turn, layer], passed.at[layer % 2], grad_send.at[side, turn, layer], passed_recv.at[layer % 2],
            (core, lat + (DETOUR + 1 if side else -DETOUR - 1)),
        )

    def passed_copy(side, part):
        to, place = (1 - core, lat - DETOUR) if side == 0 else (1 - core, lat + DETOUR)
        return [
            remote(
                passed.at[part], sides[side][6].at[core, part], passed_send.at[part], grad_recv.at[side, core, part],
                (k, place),
            )
            for k in (core, to)
        ]

    def bottom_copy(turn, part, slot):
        return remote(
            bottom.at[turn, part], own.at[slot, part], bottom_send.at[turn, part], bottom_recv.at[turn, part], partner
        )

    def pos_pass_copy():
        return remote(pos, pos_pass, pass_send.at[0], pass_recv, (core, lat - DETOUR - 1))

    def pos_passed_copies():
        return [
            remote(pos_pass, pos_next, pass_send.at[i], pos_recv.at[1], (k, lat + DETOUR))
            for i, k in enumerate((core, 1 - core))
        ]

    @pl.when(jnp.logical_and(far_prev, first))
    def _():
        pl.semaphore_signal(here_sem, inc=1, device_id=partner, device_id_type=MESH)

    @pl.when(jnp.logical_and(far_prev, second))
    def _():
        pos_pass_copy().start()

    tells = (near_prev, has_next)
    for side, _there, place, *_rest in sides:
        @pl.when(tells[side])
        def _():
            pos_copy(side, place).start()

    for load in loads:
        load.wait()

    @pl.when(jnp.logical_and(far_prev, second))
    def _():
        pl.semaphore_wait(here_sem, 1)

    for side, there, place, *_rest in sides:
        @pl.when(there)
        def _():
            full_copy(side, place).start()

    @pl.when(far_next)
    def _():
        more_copy().start()

    def own_windows(turn, carry):
        have_own[turn, core] = cut(tile, pos, 2 * turn + core, ALL)
        to_partner[turn] = cut(tile, pos, 2 * turn + 1 - core, ALL)
        part_copy(turn, core).start()
        return carry

    lax.fori_loop(0, turns, own_windows, 0)

    for side, there, place, *_rest in sides:
        @pl.when(there)
        def _():
            pos_arrival(side, place).wait_recv()

    @pl.when(jnp.logical_and(passes_down, second))
    def _():
        pos_pass_copy().wait_recv()
        for copy in pos_passed_copies():
            copy.start()

    def send_windows(turn, carry):
        for k in range(2):
            slot = 2 * turn + k
            for side, there, place, where, *_rest in sides:
                @pl.when(there)
                def _():
                    (to_prev, to_next)[side][slot] = cut(tile, where, slot, REST)

                for at_home, to in ((core == k, core), (core != k, 1 - core)):
                    when_near_or_far(
                        side, jnp.logical_and(there, at_home), far_next,
                        lambda begin: win_copy(side, turn, to, place, begin).start(),
                    )

        return carry

    lax.fori_loop(0, turns, send_windows, 0)

    def early_windows(turn, carry):
        for side, there, place, _where, full, have, _arrived in sides:
            @pl.when(there)
            def _():
                have[turn, core, :, :, FIRST] = cut(full, pos, 2 * turn + core, FIRST)
                (early_prev, early_next)[side][turn] = cut(full, pos, 2 * turn + 1 - core, FIRST)
                early_copy(side, turn, core).start()

        return carry

    for side, there, place, *_rest in sides:
        @pl.when(there)
        def _():
            full_arrival(side, place).wait_recv()

    lax.fori_loop(0, turns, early_windows, 0)

    @pl.when(far_prev)
    def _():
        more_arrival().wait_recv()

        def extra_windows(turn, carry):
            have_prev[turn, core, :, :, SECOND] = cut(more_prev, pos, 2 * turn + core, FIRST)
            early_more[turn] = cut(more_prev, pos, 2 * turn + 1 - core, FIRST)
            extra_copy(turn, core).start()
            return carry

        lax.fori_loop(0, turns, extra_windows, 0)

    for load in tables_in:
        load.wait()

    def build_window(turn, group):
        for side, there, place, *_rest in sides:
            when_near_or_far(
                1 - side, there, far_prev, lambda begin: win_arrival(side, turn, group, place, begin).wait_recv()
            )

        @pl.when(core != group)
        def _():
            part_copy(turn, group).wait_recv()
            for side, there, place, *_rest in sides:
                @pl.when(there)
                def _():
                    early_copy(side, turn, group).wait_recv()

            @pl.when(far_prev)
            def _():
                extra_copy(turn, group).wait_recv()

        row = pos[0, 2 * turn + core] - lat * HALF
        rows = lax.broadcasted_iota(jnp.int32, (2, 2, HALF, WIN), 2)
        window[group, :, :, :HALF] = jnp.where(rows >= row, have_prev[turn, group], have_next[turn, group])
        window[group, :, :, HALF:] = have_own[turn, group]

    def times(layer, re, im):
        t_re, t_im = window[layer // 2, 0, layer % 2], window[layer // 2, 1, layer % 2]
        return re * t_re - im * t_im, re * t_im + im * t_re

    def times_conj(layer, re, im):
        t_re, t_im = window[layer // 2, 0, layer % 2], window[layer // 2, 1, layer % 2]
        return re * t_re + im * t_im, im * t_re - re * t_im

    def send_term(turn, layer, re, im):
        p_re, p_im = waves[layer, 0], waves[layer, 1]
        term_re = p_re * re + p_im * im
        term_im = p_re * im - p_im * re
        top[turn, layer, 0] = term_re[:HALF]
        top[turn, layer, 1] = term_im[:HALF]
        slot = 2 * turn + core
        group, part = layer // 2, layer % 2
        for at_home, to in ((core == group, core), (core != group, 1 - core)):
            for side, there, place, *_rest in sides:
                goes = jnp.logical_and(there, at_home)
                if layer in DETOURED:
                    around = jnp.logical_and((far_prev, far_next)[side], turn == 0)

                    @pl.when(jnp.logical_and(goes, around))
                    def _():
                        detour_copy(side, turn, layer).start()

                    goes = jnp.logical_and(goes, jnp.logical_not(around))

                @pl.when(goes)
                def _():
                    grad_copy(side, turn, layer, to, place).start()

        @pl.when(core == group)
        def _():
            own[slot, part, 0] = term_re[HALF:]
            own[slot, part, 1] = term_im[HALF:]

        @pl.when(core != group)
        def _():
            bottom[turn, part, 0] = term_re[HALF:]
            bottom[turn, part, 1] = term_im[HALF:]
            bottom_copy(turn, part, slot).start()

    def whole(turn, carry):
        slot = 2 * turn + core
        row = pos[0, slot] - lat * HALF
        _, lane = column_block(pos, slot)
        re = pltpu.roll(pltpu.roll(probe[0], row, 0), lane, 1)
        im = pltpu.roll(pltpu.roll(probe[1], row, 0), lane, 1)
        for layer in range(4):
            if layer % 2 == 0:
                build_window(turn, layer // 2)
            waves[layer, 0] = re
            waves[layer, 1] = im
            re, im = product(mats, PROP if layer < 3 else DFT, *times(layer, re, im))
        live = jnp.where(slot < counts[0], 1.0, 0.0).astype(jnp.float32)
        weight = live * (1.0 - amp[slot] / jnp.sqrt(re * re + im * im + 1.0))
        re, im = product(mats, DFT_CONJ, weight * re, weight * im)
        for layer in range(3, -1, -1):
            send_term(turn, layer, re, im)
            if layer > 0:
                re, im = product(mats, PROP_CONJ, *times_conj(layer, re, im))
        return carry

    lax.fori_loop(0, turns, whole, 0)

    for side, flag in ((0, passes_up), (1, passes_down)):
        for part in [layer % 2 for layer in DETOURED]:
            @pl.when(flag)
            def _():
                pltpu.make_async_remote_copy(
                    src_ref=top.at[0, 0], dst_ref=passed.at[part], send_sem=grad_send.at[side, 0, 0],
                    recv_sem=passed_recv.at[part], device_id=partner, device_id_type=MESH,
                ).wait_recv()

            same, other = passed_copy(side, part)

            @pl.when(jnp.logical_and(flag, core == 1))
            def _():
                same.start()

            @pl.when(jnp.logical_and(flag, core == 0))
            def _():
                other.start()

    rows = lax.broadcasted_iota(jnp.int32, (2, HALF, WIN), 1)
    lanes = lax.broadcasted_iota(jnp.int32, (2, HALF, WIN), 2)

    def add(where, slot, part, piece):
        begin = where[1, slot] - HALF
        for k in range(blocks):
            offset = lanes + (k * WIN - begin)
            inside = jnp.logical_and(offset >= 0, offset < WIN)
            grad[:, part, :, k * WIN : (k + 1) * WIN] += jnp.where(inside, piece, 0.0)

    def add_own(turn, carry):
        for k in range(2):
            slot = 2 * turn + k
            for part in range(2):
                @pl.when(core != k)
                def _():
                    bottom_copy(turn, part, slot).wait_recv()

                add(pos, slot, part, own[slot, part])
        return carry

    def add_other(slot, part, side, when):
        _, _there, place, where, _full, _have, arrived = sides[side]

        @pl.when(when)
        def _():
            grad_arrival(side, slot, part, place).wait_recv()
            row = where[0, slot] - place * HALF
            keep = rows < row if side == 0 else rows >= row
            add(where, slot, part, jnp.where(keep, arrived[slot, part], 0.0))

    detoured = [layer % 2 for layer in DETOURED]
    by_detour = [jnp.logical_and(flag, core == 1) for flag in (far_prev, far_next)]

    def add_others(slot, carry):
        for part in (1, 0):
            for side, there, *_rest in sides:
                if part in detoured:
                    there = jnp.logical_and(there, jnp.logical_not(jnp.logical_and(by_detour[side], slot < 2)))
                add_other(slot, part, side, there)
        return carry

    def add_detoured(slot, carry):
        for part in detoured:
            for side in range(2):
                add_other(slot, part, side, by_detour[side])
        return carry

    lax.fori_loop(0, turns, add_own, 0)
    lax.fori_loop(0, slots, add_others, 0)
    if DETOURED:
        lax.fori_loop(0, 2, add_detoured, 0)

    for side, there, place, *_rest in sides:
        @pl.when(there)
        def _():
            full_copy(side, place).wait_send()

        @pl.when(tells[side])
        def _():
            pos_copy(side, place).wait_send()

    @pl.when(jnp.logical_and(far_prev, second))
    def _():
        pos_pass_copy().wait_send()

    @pl.when(jnp.logical_and(passes_down, second))
    def _():
        for copy in pos_passed_copies():
            copy.wait_send()

    @pl.when(far_next)
    def _():
        more_copy().wait_send()

    def finish(turn, carry):
        part_copy(turn, core).wait_send()
        for part in range(2):
            bottom_copy(turn, part, 2 * turn + 1 - core).wait_send()
        for side, there, place, *_rest in sides:
            @pl.when(there)
            def _():
                early_copy(side, turn, core).wait_send()
                for layer in range(4):
                    grad_copy(side, turn, layer, core, place).wait_send()

            for to in (core, 1 - core):
                when_near_or_far(
                    side, there, far_next, lambda begin: win_copy(side, turn, to, place, begin).wait_send()
                )

        @pl.when(far_prev)
        def _():
            extra_copy(turn, core).wait_send()

        return carry

    lax.fori_loop(0, turns, finish, 0)

    @pl.when(passes)
    def _():
        for layer in DETOURED:
            passed_copy(0, layer % 2)[0].wait_send()


def on_device(n, trans, probe, amp, pos, counts):
    slots = pos.shape[0]
    turns = slots // 2
    pos = pos.T
    blocks = trans.shape[3] // WIN
    vmem = pl.BlockSpec(memory_space=pltpu.VMEM)
    hbm = pl.BlockSpec(memory_space=pltpu.HBM)
    f32 = jnp.float32
    piece = (slots, 2, 2, HALF, WIN)
    mats = jnp.asarray(tables())
    held = [pltpu.with_memory_space_constraint(x, pltpu.HBM) for x in (pos, trans, probe, amp, mats)]
    sem = pltpu.SemaphoreType.DMA
    return pl.pallas_call(
        functools.partial(kernel, n),
        out_shape=pltpu.VMEM(trans.shape, f32),
        in_specs=[hbm] * 6,
        out_specs=vmem,
        scratch_shapes=[
            pltpu.VMEM((blocks + 2, 2, 2, HALF, WIN), f32),
            pltpu.VMEM(probe.shape, f32),
            pltpu.VMEM(amp.shape, f32),
            pltpu.VMEM(mats.shape, jnp.bfloat16),
            pltpu.VMEM((blocks + 2, 2, 2, EARLY, WIN), f32),
            pltpu.VMEM((blocks + 2, 2, 2, EARLY, WIN), f32),
            pltpu.VMEM((blocks + 2, 2, 2, EARLY, WIN), f32),
            pltpu.VMEM((slots, 2, 2, HALF - EARLY, WIN), f32),
            pltpu.VMEM((slots, 2, 2, HALF - EARLY, WIN), f32),
            pltpu.VMEM((turns, 2, 2, HALF, WIN), f32),
            pltpu.VMEM((turns, 2, 2, EARLY, WIN), f32),
            pltpu.VMEM((turns, 2, 2, EARLY, WIN), f32),
            pltpu.VMEM((turns, 2, 2, EARLY, WIN), f32),
            pltpu.VMEM((turns, 2, 2, 2, HALF, WIN), f32),
            pltpu.VMEM((turns, 2, 2, 2, HALF, WIN), f32),
            pltpu.VMEM((turns, 2, 2, 2, HALF, WIN), f32),
            pltpu.VMEM(piece, f32),
            pltpu.VMEM(piece, f32),
            pltpu.VMEM(piece, f32),
            pltpu.VMEM((2, 2, 2, WIN, WIN), f32),
            pltpu.VMEM((4, 2, WIN, WIN), f32),
            pltpu.VMEM((turns, 4, 2, HALF, WIN), f32),
            pltpu.VMEM((turns, 2, 2, HALF, WIN), f32),
            pltpu.VMEM((2, 2, HALF, WIN), f32),
            pltpu.SMEM(pos.shape, jnp.int32),
            pltpu.SMEM(counts.shape, jnp.int32),
            pltpu.SMEM(pos.shape, jnp.int32),
            pltpu.SMEM(pos.shape, jnp.int32),
            pltpu.SMEM(pos.shape, jnp.int32),
            pltpu.SemaphoreType.REGULAR,
            sem((blocks,)),
            sem((3,)),
            sem((2,)),
            sem((2,)),
            sem((2,)),
            sem((2,)),
            sem((2,)),
            sem((2, turns)),
            sem((2, turns)),
            sem(()),
            sem(()),
            sem((turns,)),
            sem((turns,)),
            sem((turns,)),
            sem((turns,)),
            sem((2, slots)),
            sem((2, turns, 2)),
            sem((2, turns, 4)),
            sem((2, slots, 2)),
            sem((turns, 2)),
            sem((turns, 2)),
            sem((2,)),
            sem((2,)),
            sem((2,)),
            sem(()),
        ],
        compiler_params=pltpu.CompilerParams(
            collective_id=0, has_side_effects=True, vmem_limit_bytes=40 << 20
        ),
        name="windows",
    )(held[0], counts, *held[1:])


def solution(mesh):
    placed = (P(None, "depth", "lat", None), P(), P("lat", None, None), P("lat", None), P("lat"))
    return jax.shard_map(
        functools.partial(on_device, mesh.shape["lat"]),
        mesh=mesh,
        in_specs=placed,
        out_specs=P(None, "depth", "lat", None),
        check_vma=False,
    )
```

```python
import functools

import jax
import jax.numpy as jnp
import ml_dtypes
import numpy as np
from jax import lax
from jax.experimental import pallas as pl
from jax.experimental.pallas import tpu as pltpu
from jax.sharding import PartitionSpec as P

PROP_COEF = 40.0
WIN = 128
HALF = 64
EARLY = 8
PLANE = 16
DETOUR = 3
MESH = pl.DeviceIdType.MESH
PROP, PROP_CONJ, DFT, DFT_CONJ = range(4)


def tables():
    index = np.arange(WIN)
    dft = np.exp(-2j * np.pi * (np.outer(index, index) % WIN) / WIN) / np.sqrt(WIN)
    freq = ((index + WIN // 2) % WIN - WIN // 2) / WIN
    prop = dft.conj() @ np.diag(np.exp(-1j * PROP_COEF * freq * freq)) @ dft
    terms = []
    for matrix in (prop, prop.conj(), dft, dft.conj()):
        real = np.block([[matrix.real, -matrix.imag], [matrix.imag, matrix.real]])
        high = real.astype(ml_dtypes.bfloat16)
        low = (real - high.astype(np.float64)).astype(ml_dtypes.bfloat16)
        terms.append(np.stack([high, low]))
    return np.stack(terms)


def split(values):
    high = values.astype(jnp.bfloat16)
    low = (values - high.astype(jnp.float32)).astype(jnp.bfloat16)
    return high, low


def product(mats, which, re, im):
    conj = which ^ 1
    high, low = split(jnp.concatenate([re, im], axis=1))
    right = jnp.concatenate([mats[conj, 0], mats[conj, 0], mats[conj, 1]], axis=0)
    first = jnp.dot(
        jnp.concatenate([high, low, high], axis=1), right, preferred_element_type=jnp.float32
    )
    high, low = split(first)
    left = jnp.concatenate(
        [mats[which, 0, :, :WIN], mats[which, 0, :, :WIN], mats[which, 1, :, :WIN]], axis=1
    )
    second = jnp.dot(
        left, jnp.concatenate([high, low, high], axis=0), preferred_element_type=jnp.float32
    )
    return second[:WIN, :WIN] - second[WIN:, WIN:], second[:WIN, WIN:] + second[WIN:, :WIN]


def column_block(pos, slot):
    column = pos[1, slot] + HALF
    return lax.shift_right_logical(column, 7), column & (WIN - 1)


def cut(tile, pos, slot, rows):
    block, lane = column_block(pos, slot)
    first, second = tile[block, :, :, rows], tile[block + 1, :, :, rows]
    lanes = lax.broadcasted_iota(jnp.int32, first.shape, 3)
    return jnp.where(lanes >= lane, first, second)


DETOURED = (3,)
ALL = slice(0, HALF)
FIRST = slice(0, EARLY)
SECOND = slice(EARLY, 2 * EARLY)
REST = slice(EARLY, HALF)


def kernel(
    n, pos_hbm, counts_hbm, trans, probe_hbm, amp_hbm, mats_hbm,
    grad,
    tile, probe, amp, mats, full_prev, full_next, more_prev, to_prev, to_next, to_partner, early_prev, early_next, early_more,
    have_prev, have_next, have_own, from_prev, from_next, own, window, waves, top, bottom, passed, pos, counts, pos_prev, pos_next, pos_pass,
    here_sem, tile_sem, table_sem, pos_sem, pos_send, pos_recv, full_send, full_recv, early_send, early_recv,
    more_send, more_recv, extra_send, extra_recv,
    part_send, part_recv, win_send, win_recv, grad_send, grad_recv, bottom_send, bottom_recv, passed_send, passed_recv, pass_send, pass_recv,
):
    core = lax.axis_index("depth")
    lat = lax.axis_index("lat")
    has_prev = lat > 0
    has_next = lat < n - 1
    far_prev = jnp.logical_and(has_prev, lax.rem(lat, PLANE) == 0)
    far_next = jnp.logical_and(has_next, lax.rem(lat, PLANE) == PLANE - 1)
    first_of_plane, last_of_plane = lat - DETOUR, lat + DETOUR
    passes_up = jnp.logical_and(first_of_plane > 0, lax.rem(first_of_plane, PLANE) == 0)
    passes_down = jnp.logical_and(last_of_plane < n - 1, lax.rem(last_of_plane, PLANE) == PLANE - 1)
    passes = jnp.logical_or(passes_up, passes_down)
    slots = pos.shape[1]
    turns = slots // 2
    blocks = tile.shape[0] - 2
    partner = (1 - core, lat)
    sides = (
        (0, has_prev, lat - 1, pos_prev, full_prev, have_prev, from_prev),
        (1, has_next, lat + 1, pos_next, full_next, have_next, from_next),
    )

    scalars = [
        pltpu.make_async_copy(source, target, pos_sem.at[k])
        for k, (source, target) in enumerate(((pos_hbm, pos), (counts_hbm, counts)))
    ]
    loads = [
        pltpu.make_async_copy(
            trans.at[:, :, :, pl.ds(k * WIN, WIN)], tile.at[k + 1], tile_sem.at[k]
        )
        for k in range(blocks)
    ]
    tables_in = [
        pltpu.make_async_copy(source, target, table_sem.at[k])
        for k, (source, target) in enumerate(((mats_hbm, mats), (probe_hbm, probe), (amp_hbm, amp)))
    ]
    for load in scalars + loads + tables_in:
        load.start()

    barrier = pltpu.get_barrier_semaphore()
    near_prev = jnp.logical_and(has_prev, jnp.logical_not(far_prev))
    near_next = jnp.logical_and(has_next, jnp.logical_not(far_next))
    first, second = core == 0, core == 1
    to_same = ((has_prev, lat - 1), (jnp.logical_or(near_next, jnp.logical_and(far_next, first)), lat + 1))
    to_other = ((has_prev, lat - 1), (jnp.logical_or(near_next, jnp.logical_and(far_next, second)), lat + 1))
    for targets, k in ((to_same, core), (to_other, 1 - core)):
        for there, place in targets:
            @pl.when(there)
            def _():
                pl.semaphore_signal(barrier, inc=1, device_id=(k, place), device_id_type=MESH)

    pl.semaphore_signal(barrier, inc=1, device_id=partner, device_id_type=MESH)

    @pl.when(passes_up)
    def _():
        pl.semaphore_signal(barrier, inc=1, device_id=(core, lat - DETOUR - 1), device_id_type=MESH)

    @pl.when(passes_down)
    def _():
        pl.semaphore_signal(barrier, inc=1, device_id=(core, lat + DETOUR + 1), device_id_type=MESH)

    @pl.when(jnp.logical_and(far_next, first))
    def _():
        pl.semaphore_signal(barrier, inc=1, device_id=(1 - core, lat - DETOUR), device_id_type=MESH)

    for flag, place in ((far_prev, lat + DETOUR), (far_next, lat - DETOUR)):
        @pl.when(jnp.logical_and(flag, core == 1))
        def _():
            for k in (core, 1 - core):
                pl.semaphore_signal(barrier, inc=1, device_id=(k, place), device_id_type=MESH)

    grad[...] = jnp.zeros_like(grad)
    for padded in (tile, full_prev, full_next, more_prev):
        padded[0] = jnp.zeros(padded.shape[1:], jnp.float32)
        padded[blocks + 1] = jnp.zeros(padded.shape[1:], jnp.float32)
    for _, there, _place, where, full, have, _arrived in sides:
        @pl.when(jnp.logical_not(there))
        def _():
            have[...] = jnp.zeros_like(have)
            for k in range(slots):
                where[0, k] = 0
                where[1, k] = 0

    for load in scalars:
        load.wait()
    pl.semaphore_wait(
        barrier,
        1 + 2 * jnp.logical_or(near_prev, jnp.logical_and(far_prev, first)).astype(jnp.int32)
        + 2 * has_next.astype(jnp.int32) + jnp.logical_and(passes_down, second).astype(jnp.int32)
        + far_prev.astype(jnp.int32) + far_next.astype(jnp.int32) + passes.astype(jnp.int32),
    )

    def remote(source, target, send, recv, device):
        return pltpu.make_async_remote_copy(
            src_ref=source, dst_ref=target, send_sem=send, recv_sem=recv,
            device_id=device, device_id_type=MESH,
        )

    def pos_copy(side, place):
        return remote(pos, sides[1 - side][3], pos_send.at[side], pos_recv.at[1 - side], (core, place))

    def pos_arrival(side, place):
        return remote(pos, sides[side][3], pos_send.at[side], pos_recv.at[side], (core, place))

    def full_copy(side, place):
        return remote(
            tile.at[pl.ds(1, blocks), :, :, pl.ds(0, EARLY)], sides[1 - side][4].at[pl.ds(1, blocks)],
            full_send.at[side], full_recv.at[1 - side], (core, place),
        )

    def full_arrival(side, place):
        return remote(
            tile.at[pl.ds(1, blocks), :, :, pl.ds(0, EARLY)], sides[side][4].at[pl.ds(1, blocks)],
            full_send.at[side], full_recv.at[side], (core, place),
        )

    def more_copy():
        return remote(
            tile.at[pl.ds(1, blocks), :, :, pl.ds(EARLY, EARLY)], more_prev.at[pl.ds(1, blocks)],
            more_send, more_recv, (core, lat + 1),
        )

    def more_arrival():
        return remote(
            tile.at[pl.ds(1, blocks), :, :, pl.ds(EARLY, EARLY)], more_prev.at[pl.ds(1, blocks)],
            more_send, more_recv, (core, lat - 1),
        )

    def when_near_or_far(side, there, far, act):
        if side == 0:
            pl.when(there)(functools.partial(act, EARLY))
        else:
            pl.when(jnp.logical_and(there, jnp.logical_not(far)))(functools.partial(act, EARLY))
            pl.when(jnp.logical_and(there, far))(functools.partial(act, 2 * EARLY))

    def win_copy(side, turn, to, place, begin):
        slot, rows = 2 * turn + to, HALF - begin
        return remote(
            (to_prev, to_next)[side].at[slot, :, :, pl.ds(begin - EARLY, rows)],
            sides[1 - side][5].at[turn, core, :, :, pl.ds(begin, rows)],
            win_send.at[side, slot], win_recv.at[1 - side, turn, core], (to, place),
        )

    def win_arrival(side, turn, group, place, begin):
        rows = HALF - begin
        return remote(
            to_prev.at[0, :, :, pl.ds(begin - EARLY, rows)], sides[side][5].at[turn, group, :, :, pl.ds(begin, rows)],
            win_send.at[side, 0], win_recv.at[side, turn, group], (core, place),
        )

    def extra_copy(turn, group):
        return remote(
            early_more.at[turn], have_prev.at[turn, group, :, :, pl.ds(EARLY, EARLY)],
            extra_send.at[turn], extra_recv.at[turn], partner,
        )

    def early_copy(side, turn, group):
        return remote(
            (early_prev, early_next)[side].at[turn], sides[side][5].at[turn, group, :, :, pl.ds(0, EARLY)],
            early_send.at[side, turn], early_recv.at[side, turn], partner,
        )

    def part_copy(turn, group):
        return remote(
            to_partner.at[turn], have_own.at[turn, group], part_send.at[turn], part_recv.at[turn], partner
        )

    def grad_copy(side, turn, layer, to, place):
        slot = 2 * turn + core
        return remote(
            top.at[turn, layer], sides[1 - side][6].at[slot, layer % 2],
            grad_send.at[side, turn, layer], grad_recv.at[1 - side, slot, layer % 2], (to, place),
        )

    def grad_arrival(side, slot, part, place):
        return remote(
            top.at[0, 0], sides[side][6].at[slot, part],
            grad_send.at[side, 0, 0], grad_recv.at[side, slot, part], (core, place),
        )

    def detour_copy(side, turn, layer):
        return remote(
            top.at[turn, layer], passed.at[layer % 2], grad_send.at[side, turn, layer], passed_recv.at[layer % 2],
            (core, lat + (DETOUR + 1 if side else -DETOUR - 1)),
        )

    def passed_copy(side, part):
        to, place = (1 - core, lat - DETOUR) if side == 0 else (1 - core, lat + DETOUR)
        return [
            remote(
                passed.at[part], sides[side][6].at[2 + core, part], passed_send.at[part], grad_recv.at[side, 2 + core, part],
                (k, place),
            )
            for k in (core, to)
        ]

    def bottom_copy(turn, part, slot):
        return remote(
            bottom.at[turn, part], own.at[slot, part], bottom_send.at[turn, part], bottom_recv.at[turn, part], partner
        )

    def pos_pass_copy():
        return remote(pos, pos_pass, pass_send.at[0], pass_recv, (core, lat - DETOUR - 1))

    def pos_passed_copies():
        return [
            remote(pos_pass, pos_next, pass_send.at[i], pos_recv.at[1], (k, lat + DETOUR))
            for i, k in enumerate((core, 1 - core))
        ]

    @pl.when(jnp.logical_and(far_prev, first))
    def _():
        pl.semaphore_signal(here_sem, inc=1, device_id=partner, device_id_type=MESH)

    @pl.when(jnp.logical_and(far_prev, second))
    def _():
        pos_pass_copy().start()

    tells = (near_prev, has_next)
    for side, _there, place, *_rest in sides:
        @pl.when(tells[side])
        def _():
            pos_copy(side, place).start()

    for load in loads:
        load.wait()

    @pl.when(jnp.logical_and(far_prev, second))
    def _():
        pl.semaphore_wait(here_sem, 1)

    for side, there, place, *_rest in sides:
        @pl.when(there)
        def _():
            full_copy(side, place).start()

    @pl.when(far_next)
    def _():
        more_copy().start()

    def own_windows(turn, carry):
        have_own[turn, core] = cut(tile, pos, 2 * turn + core, ALL)
        to_partner[turn] = cut(tile, pos, 2 * turn + 1 - core, ALL)
        part_copy(turn, core).start()
        return carry

    lax.fori_loop(0, turns, own_windows, 0)

    for side, there, place, *_rest in sides:
        @pl.when(there)
        def _():
            pos_arrival(side, place).wait_recv()

    @pl.when(jnp.logical_and(passes_down, second))
    def _():
        pos_pass_copy().wait_recv()
        for copy in pos_passed_copies():
            copy.start()

    def send_windows(turn, carry):
        for k in range(2):
            slot = 2 * turn + k
            for side, there, place, where, *_rest in sides:
                @pl.when(there)
                def _():
                    (to_prev, to_next)[side][slot] = cut(tile, where, slot, REST)

                for at_home, to in ((core == k, core), (core != k, 1 - core)):
                    when_near_or_far(
                        side, jnp.logical_and(there, at_home), far_next,
                        lambda begin: win_copy(side, turn, to, place, begin).start(),
                    )

        return carry

    lax.fori_loop(0, turns, send_windows, 0)

    def early_windows(turn, carry):
        for side, there, place, _where, full, have, _arrived in sides:
            @pl.when(there)
            def _():
                have[turn, core, :, :, FIRST] = cut(full, pos, 2 * turn + core, FIRST)
                (early_prev, early_next)[side][turn] = cut(full, pos, 2 * turn + 1 - core, FIRST)
                early_copy(side, turn, core).start()

        return carry

    for side, there, place, *_rest in sides:
        @pl.when(there)
        def _():
            full_arrival(side, place).wait_recv()

    lax.fori_loop(0, turns, early_windows, 0)

    @pl.when(far_prev)
    def _():
        more_arrival().wait_recv()

        def extra_windows(turn, carry):
            have_prev[turn, core, :, :, SECOND] = cut(more_prev, pos, 2 * turn + core, FIRST)
            early_more[turn] = cut(more_prev, pos, 2 * turn + 1 - core, FIRST)
            extra_copy(turn, core).start()
            return carry

        lax.fori_loop(0, turns, extra_windows, 0)

    for load in tables_in:
        load.wait()

    def build_window(turn, group):
        for side, there, place, *_rest in sides:
            when_near_or_far(
                1 - side, there, far_prev, lambda begin: win_arrival(side, turn, group, place, begin).wait_recv()
            )

        @pl.when(core != group)
        def _():
            part_copy(turn, group).wait_recv()
            for side, there, place, *_rest in sides:
                @pl.when(there)
                def _():
                    early_copy(side, turn, group).wait_recv()

            @pl.when(far_prev)
            def _():
                extra_copy(turn, group).wait_recv()

        row = pos[0, 2 * turn + core] - lat * HALF
        rows = lax.broadcasted_iota(jnp.int32, (2, 2, HALF, WIN), 2)
        window[group, :, :, :HALF] = jnp.where(rows >= row, have_prev[turn, group], have_next[turn, group])
        window[group, :, :, HALF:] = have_own[turn, group]

    def times(layer, re, im):
        t_re, t_im = window[layer // 2, 0, layer % 2], window[layer // 2, 1, layer % 2]
        return re * t_re - im * t_im, re * t_im + im * t_re

    def times_conj(layer, re, im):
        t_re, t_im = window[layer // 2, 0, layer % 2], window[layer // 2, 1, layer % 2]
        return re * t_re + im * t_im, im * t_re - re * t_im

    def send_term(turn, layer, re, im):
        p_re, p_im = waves[layer, 0], waves[layer, 1]
        term_re = p_re * re + p_im * im
        term_im = p_re * im - p_im * re
        top[turn, layer, 0] = term_re[:HALF]
        top[turn, layer, 1] = term_im[:HALF]
        slot = 2 * turn + core
        group, part = layer // 2, layer % 2
        for at_home, to in ((core == group, core), (core != group, 1 - core)):
            for side, there, place, *_rest in sides:
                goes = jnp.logical_and(there, at_home)
                if layer in DETOURED:
                    around = jnp.logical_and((far_prev, far_next)[side], turn == 1)

                    @pl.when(jnp.logical_and(goes, around))
                    def _():
                        detour_copy(side, turn, layer).start()

                    goes = jnp.logical_and(goes, jnp.logical_not(around))

                @pl.when(goes)
                def _():
                    grad_copy(side, turn, layer, to, place).start()

        @pl.when(core == group)
        def _():
            own[slot, part, 0] = term_re[HALF:]
            own[slot, part, 1] = term_im[HALF:]

        @pl.when(core != group)
        def _():
            bottom[turn, part, 0] = term_re[HALF:]
            bottom[turn, part, 1] = term_im[HALF:]
            bottom_copy(turn, part, slot).start()

    def whole(turn, carry):
        slot = 2 * turn + core
        row = pos[0, slot] - lat * HALF
        _, lane = column_block(pos, slot)
        re = pltpu.roll(pltpu.roll(probe[0], row, 0), lane, 1)
        im = pltpu.roll(pltpu.roll(probe[1], row, 0), lane, 1)
        for layer in range(4):
            if layer % 2 == 0:
                build_window(turn, layer // 2)
            waves[layer, 0] = re
            waves[layer, 1] = im
            re, im = product(mats, PROP if layer < 3 else DFT, *times(layer, re, im))
        live = jnp.where(slot < counts[0], 1.0, 0.0).astype(jnp.float32)
        weight = live * (1.0 - amp[slot] / jnp.sqrt(re * re + im * im + 1.0))
        re, im = product(mats, DFT_CONJ, weight * re, weight * im)
        for layer in range(3, -1, -1):
            send_term(turn, layer, re, im)
            if layer > 0:
                re, im = product(mats, PROP_CONJ, *times_conj(layer, re, im))
        return carry

    lax.fori_loop(0, turns, whole, 0)

    rows = lax.broadcasted_iota(jnp.int32, (2, HALF, WIN), 1)
    lanes = lax.broadcasted_iota(jnp.int32, (2, HALF, WIN), 2)

    def add(where, slot, part, piece):
        begin = where[1, slot] - HALF
        for k in range(blocks):
            offset = lanes + (k * WIN - begin)
            inside = jnp.logical_and(offset >= 0, offset < WIN)
            grad[:, part, :, k * WIN : (k + 1) * WIN] += jnp.where(inside, piece, 0.0)

    def add_own(turn, carry):
        for k in range(2):
            slot = 2 * turn + k
            for part in range(2):
                @pl.when(core != k)
                def _():
                    bottom_copy(turn, part, slot).wait_recv()

                add(pos, slot, part, own[slot, part])
        return carry

    def add_other(slot, part, side, when):
        _, _there, place, where, _full, _have, arrived = sides[side]

        @pl.when(when)
        def _():
            grad_arrival(side, slot, part, place).wait_recv()
            row = where[0, slot] - place * HALF
            keep = rows < row if side == 0 else rows >= row
            add(where, slot, part, jnp.where(keep, arrived[slot, part], 0.0))

    detoured = [layer % 2 for layer in DETOURED]
    by_detour = [jnp.logical_and(flag, core == 1) for flag in (far_prev, far_next)]

    def add_others(slot, carry):
        for part in (1, 0):
            for side, there, *_rest in sides:
                if part in detoured:
                    there = jnp.logical_and(there, jnp.logical_not(jnp.logical_and(by_detour[side], slot >= 2)))
                add_other(slot, part, side, there)
        return carry

    def add_detoured(slot, carry):
        for part in detoured:
            for side in range(2):
                add_other(slot, part, side, by_detour[side])
        return carry

    lax.fori_loop(0, turns, add_own, 0)
    lax.fori_loop(0, 2, add_others, 0)

    for side, flag in ((0, passes_up), (1, passes_down)):
        for part in [layer % 2 for layer in DETOURED]:
            @pl.when(flag)
            def _():
                pltpu.make_async_remote_copy(
                    src_ref=top.at[0, 0], dst_ref=passed.at[part], send_sem=grad_send.at[side, 0, 0],
                    recv_sem=passed_recv.at[part], device_id=partner, device_id_type=MESH,
                ).wait_recv()

            same, other = passed_copy(side, part)

            @pl.when(jnp.logical_and(flag, core == 1))
            def _():
                same.start()

            @pl.when(jnp.logical_and(flag, core == 0))
            def _():
                other.start()

    lax.fori_loop(2, slots, add_others, 0)
    if DETOURED:
        lax.fori_loop(2, slots, add_detoured, 0)

    for side, there, place, *_rest in sides:
        @pl.when(there)
        def _():
            full_copy(side, place).wait_send()

        @pl.when(tells[side])
        def _():
            pos_copy(side, place).wait_send()

    @pl.when(jnp.logical_and(far_prev, second))
    def _():
        pos_pass_copy().wait_send()

    @pl.when(jnp.logical_and(passes_down, second))
    def _():
        for copy in pos_passed_copies():
            copy.wait_send()

    @pl.when(far_next)
    def _():
        more_copy().wait_send()

    def finish(turn, carry):
        part_copy(turn, core).wait_send()
        for part in range(2):
            bottom_copy(turn, part, 2 * turn + 1 - core).wait_send()
        for side, there, place, *_rest in sides:
            @pl.when(there)
            def _():
                early_copy(side, turn, core).wait_send()
                for layer in range(4):
                    grad_copy(side, turn, layer, core, place).wait_send()

            for to in (core, 1 - core):
                when_near_or_far(
                    side, there, far_next, lambda begin: win_copy(side, turn, to, place, begin).wait_send()
                )

        @pl.when(far_prev)
        def _():
            extra_copy(turn, core).wait_send()

        return carry

    lax.fori_loop(0, turns, finish, 0)

    @pl.when(passes)
    def _():
        for layer in DETOURED:
            passed_copy(0, layer % 2)[0].wait_send()


def on_device(n, trans, probe, amp, pos, counts):
    slots = pos.shape[0]
    turns = slots // 2
    pos = pos.T
    blocks = trans.shape[3] // WIN
    vmem = pl.BlockSpec(memory_space=pltpu.VMEM)
    hbm = pl.BlockSpec(memory_space=pltpu.HBM)
    f32 = jnp.float32
    piece = (slots, 2, 2, HALF, WIN)
    mats = jnp.asarray(tables())
    held = [pltpu.with_memory_space_constraint(x, pltpu.HBM) for x in (pos, trans, probe, amp, mats)]
    sem = pltpu.SemaphoreType.DMA
    return pl.pallas_call(
        functools.partial(kernel, n),
        out_shape=pltpu.VMEM(trans.shape, f32),
        in_specs=[hbm] * 6,
        out_specs=vmem,
        scratch_shapes=[
            pltpu.VMEM((blocks + 2, 2, 2, HALF, WIN), f32),
            pltpu.VMEM(probe.shape, f32),
            pltpu.VMEM(amp.shape, f32),
            pltpu.VMEM(mats.shape, jnp.bfloat16),
            pltpu.VMEM((blocks + 2, 2, 2, EARLY, WIN), f32),
            pltpu.VMEM((blocks + 2, 2, 2, EARLY, WIN), f32),
            pltpu.VMEM((blocks + 2, 2, 2, EARLY, WIN), f32),
            pltpu.VMEM((slots, 2, 2, HALF - EARLY, WIN), f32),
            pltpu.VMEM((slots, 2, 2, HALF - EARLY, WIN), f32),
            pltpu.VMEM((turns, 2, 2, HALF, WIN), f32),
            pltpu.VMEM((turns, 2, 2, EARLY, WIN), f32),
            pltpu.VMEM((turns, 2, 2, EARLY, WIN), f32),
            pltpu.VMEM((turns, 2, 2, EARLY, WIN), f32),
            pltpu.VMEM((turns, 2, 2, 2, HALF, WIN), f32),
            pltpu.VMEM((turns, 2, 2, 2, HALF, WIN), f32),
            pltpu.VMEM((turns, 2, 2, 2, HALF, WIN), f32),
            pltpu.VMEM(piece, f32),
            pltpu.VMEM(piece, f32),
            pltpu.VMEM(piece, f32),
            pltpu.VMEM((2, 2, 2, WIN, WIN), f32),
            pltpu.VMEM((4, 2, WIN, WIN), f32),
            pltpu.VMEM((turns, 4, 2, HALF, WIN), f32),
            pltpu.VMEM((turns, 2, 2, HALF, WIN), f32),
            pltpu.VMEM((2, 2, HALF, WIN), f32),
            pltpu.SMEM(pos.shape, jnp.int32),
            pltpu.SMEM(counts.shape, jnp.int32),
            pltpu.SMEM(pos.shape, jnp.int32),
            pltpu.SMEM(pos.shape, jnp.int32),
            pltpu.SMEM(pos.shape, jnp.int32),
            pltpu.SemaphoreType.REGULAR,
            sem((blocks,)),
            sem((3,)),
            sem((2,)),
            sem((2,)),
            sem((2,)),
            sem((2,)),
            sem((2,)),
            sem((2, turns)),
            sem((2, turns)),
            sem(()),
            sem(()),
            sem((turns,)),
            sem((turns,)),
            sem((turns,)),
            sem((turns,)),
            sem((2, slots)),
            sem((2, turns, 2)),
            sem((2, turns, 4)),
            sem((2, slots, 2)),
            sem((turns, 2)),
            sem((turns, 2)),
            sem((2,)),
            sem((2,)),
            sem((2,)),
            sem(()),
        ],
        compiler_params=pltpu.CompilerParams(
            collective_id=0, has_side_effects=True, vmem_limit_bytes=40 << 20
        ),
        name="windows",
    )(held[0], counts, *held[1:])


def solution(mesh):
    placed = (P(None, "depth", "lat", None), P(), P("lat", None, None), P("lat", None), P("lat"))
    return jax.shard_map(
        functools.partial(on_device, mesh.shape["lat"]),
        mesh=mesh,
        in_specs=placed,
        out_specs=P(None, "depth", "lat", None),
        check_vma=False,
    )
```

```python
import functools

import jax
import jax.numpy as jnp
import ml_dtypes
import numpy as np
from jax import lax
from jax.experimental import pallas as pl
from jax.experimental.pallas import tpu as pltpu
from jax.sharding import PartitionSpec as P

PROP_COEF = 40.0
WIN = 128
HALF = 64
EARLY = 8
PLANE = 16
DETOUR = 3
MESH = pl.DeviceIdType.MESH
PROP, PROP_CONJ, DFT, DFT_CONJ = range(4)


def tables():
    index = np.arange(WIN)
    dft = np.exp(-2j * np.pi * (np.outer(index, index) % WIN) / WIN) / np.sqrt(WIN)
    freq = ((index + WIN // 2) % WIN - WIN // 2) / WIN
    prop = dft.conj() @ np.diag(np.exp(-1j * PROP_COEF * freq * freq)) @ dft
    terms = []
    for matrix in (prop, prop.conj(), dft, dft.conj()):
        real = np.block([[matrix.real, -matrix.imag], [matrix.imag, matrix.real]])
        high = real.astype(ml_dtypes.bfloat16)
        low = (real - high.astype(np.float64)).astype(ml_dtypes.bfloat16)
        terms.append(np.stack([high, low]))
    return np.stack(terms)


def split(values):
    high = values.astype(jnp.bfloat16)
    low = (values - high.astype(jnp.float32)).astype(jnp.bfloat16)
    return high, low


def product(mats, which, re, im):
    conj = which ^ 1
    high, low = split(jnp.concatenate([re, im], axis=1))
    right = jnp.concatenate([mats[conj, 0], mats[conj, 0], mats[conj, 1]], axis=0)
    first = jnp.dot(
        jnp.concatenate([high, low, high], axis=1), right, preferred_element_type=jnp.float32
    )
    high, low = split(first)
    left = jnp.concatenate(
        [mats[which, 0, :, :WIN], mats[which, 0, :, :WIN], mats[which, 1, :, :WIN]], axis=1
    )
    second = jnp.dot(
        left, jnp.concatenate([high, low, high], axis=0), preferred_element_type=jnp.float32
    )
    return second[:WIN, :WIN] - second[WIN:, WIN:], second[:WIN, WIN:] + second[WIN:, :WIN]


def column_block(pos, slot):
    column = pos[1, slot] + HALF
    return lax.shift_right_logical(column, 7), column & (WIN - 1)


def cut(tile, pos, slot, rows):
    block, lane = column_block(pos, slot)
    first, second = tile[block, :, :, rows], tile[block + 1, :, :, rows]
    lanes = lax.broadcasted_iota(jnp.int32, first.shape, 3)
    return jnp.where(lanes >= lane, first, second)


DETOURED = (3,)
ALL = slice(0, HALF)
FIRST = slice(0, EARLY)
SECOND = slice(EARLY, 2 * EARLY)
REST = slice(EARLY, HALF)


def kernel(
    n, pos_hbm, counts_hbm, trans, probe_hbm, amp_hbm, mats_hbm,
    grad,
    tile, probe, amp, mats, full_prev, full_next, more_prev, to_prev, to_next, to_partner, early_prev, early_next, early_more,
    have_prev, have_next, have_own, from_prev, from_next, own, window, waves, top, bottom, passed, pos, counts, pos_prev, pos_next, pos_pass,
    here_sem, tile_sem, table_sem, pos_sem, pos_send, pos_recv, full_send, full_recv, early_send, early_recv,
    more_send, more_recv, extra_send, extra_recv,
    part_send, part_recv, win_send, win_recv, grad_send, grad_recv, bottom_send, bottom_recv, passed_send, passed_recv, pass_send, pass_recv,
):
    core = lax.axis_index("depth")
    lat = lax.axis_index("lat")
    has_prev = lat > 0
    has_next = lat < n - 1
    far_prev = jnp.logical_and(has_prev, lax.rem(lat, PLANE) == 0)
    far_next = jnp.logical_and(has_next, lax.rem(lat, PLANE) == PLANE - 1)
    first_of_plane, last_of_plane = lat - DETOUR, lat + DETOUR
    passes_up = jnp.logical_and(first_of_plane > 0, lax.rem(first_of_plane, PLANE) == 0)
    passes_down = jnp.logical_and(last_of_plane < n - 1, lax.rem(last_of_plane, PLANE) == PLANE - 1)
    passes = jnp.logical_or(passes_up, passes_down)
    slots = pos.shape[1]
    turns = slots // 2
    blocks = tile.shape[0] - 2
    partner = (1 - core, lat)
    sides = (
        (0, has_prev, lat - 1, pos_prev, full_prev, have_prev, from_prev),
        (1, has_next, lat + 1, pos_next, full_next, have_next, from_next),
    )

    scalars = [
        pltpu.make_async_copy(source, target, pos_sem.at[k])
        for k, (source, target) in enumerate(((pos_hbm, pos), (counts_hbm, counts)))
    ]
    loads = [
        pltpu.make_async_copy(
            trans.at[:, :, :, pl.ds(k * WIN, WIN)], tile.at[k + 1], tile_sem.at[k]
        )
        for k in range(blocks)
    ]
    tables_in = [
        pltpu.make_async_copy(source, target, table_sem.at[k])
        for k, (source, target) in enumerate(((mats_hbm, mats), (probe_hbm, probe), (amp_hbm, amp)))
    ]
    for load in scalars + loads + tables_in:
        load.start()

    barrier = pltpu.get_barrier_semaphore()
    near_prev = jnp.logical_and(has_prev, jnp.logical_not(far_prev))
    near_next = jnp.logical_and(has_next, jnp.logical_not(far_next))
    first, second = core == 0, core == 1
    to_same = ((has_prev, lat - 1), (jnp.logical_or(near_next, jnp.logical_and(far_next, first)), lat + 1))
    to_other = ((has_prev, lat - 1), (jnp.logical_or(near_next, jnp.logical_and(far_next, second)), lat + 1))
    for targets, k in ((to_same, core), (to_other, 1 - core)):
        for there, place in targets:
            @pl.when(there)
            def _():
                pl.semaphore_signal(barrier, inc=1, device_id=(k, place), device_id_type=MESH)

    pl.semaphore_signal(barrier, inc=1, device_id=partner, device_id_type=MESH)

    @pl.when(passes_up)
    def _():
        pl.semaphore_signal(barrier, inc=1, device_id=(core, lat - DETOUR - 1), device_id_type=MESH)

    @pl.when(passes_down)
    def _():
        pl.semaphore_signal(barrier, inc=1, device_id=(core, lat + DETOUR + 1), device_id_type=MESH)

    @pl.when(jnp.logical_and(far_next, first))
    def _():
        pl.semaphore_signal(barrier, inc=1, device_id=(1 - core, lat - DETOUR), device_id_type=MESH)

    for flag, place in ((far_prev, lat + DETOUR), (far_next, lat - DETOUR)):
        @pl.when(jnp.logical_and(flag, core == 1))
        def _():
            for k in (core, 1 - core):
                pl.semaphore_signal(barrier, inc=1, device_id=(k, place), device_id_type=MESH)

    grad[...] = jnp.zeros_like(grad)
    for padded in (tile, full_prev, full_next, more_prev):
        padded[0] = jnp.zeros(padded.shape[1:], jnp.float32)
        padded[blocks + 1] = jnp.zeros(padded.shape[1:], jnp.float32)
    for _, there, _place, where, full, have, _arrived in sides:
        @pl.when(jnp.logical_not(there))
        def _():
            have[...] = jnp.zeros_like(have)
            for k in range(slots):
                where[0, k] = 0
                where[1, k] = 0

    for load in scalars:
        load.wait()
    pl.semaphore_wait(
        barrier,
        1 + 2 * jnp.logical_or(near_prev, jnp.logical_and(far_prev, first)).astype(jnp.int32)
        + 2 * has_next.astype(jnp.int32) + jnp.logical_and(passes_down, second).astype(jnp.int32)
        + far_prev.astype(jnp.int32) + far_next.astype(jnp.int32) + passes.astype(jnp.int32),
    )

    def remote(source, target, send, recv, device):
        return pltpu.make_async_remote_copy(
            src_ref=source, dst_ref=target, send_sem=send, recv_sem=recv,
            device_id=device, device_id_type=MESH,
        )

    def pos_copy(side, place):
        return remote(pos, sides[1 - side][3], pos_send.at[side], pos_recv.at[1 - side], (core, place))

    def pos_arrival(side, place):
        return remote(pos, sides[side][3], pos_send.at[side], pos_recv.at[side], (core, place))

    def full_copy(side, place):
        return remote(
            tile.at[pl.ds(1, blocks), :, :, pl.ds(0, EARLY)], sides[1 - side][4].at[pl.ds(1, blocks)],
            full_send.at[side], full_recv.at[1 - side], (core, place),
        )

    def full_arrival(side, place):
        return remote(
            tile.at[pl.ds(1, blocks), :, :, pl.ds(0, EARLY)], sides[side][4].at[pl.ds(1, blocks)],
            full_send.at[side], full_recv.at[side], (core, place),
        )

    def more_copy():
        return remote(
            tile.at[pl.ds(1, blocks), :, :, pl.ds(EARLY, EARLY)], more_prev.at[pl.ds(1, blocks)],
            more_send, more_recv, (core, lat + 1),
        )

    def more_arrival():
        return remote(
            tile.at[pl.ds(1, blocks), :, :, pl.ds(EARLY, EARLY)], more_prev.at[pl.ds(1, blocks)],
            more_send, more_recv, (core, lat - 1),
        )

    def when_near_or_far(side, there, far, act):
        if side == 0:
            pl.when(there)(functools.partial(act, EARLY))
        else:
            pl.when(jnp.logical_and(there, jnp.logical_not(far)))(functools.partial(act, EARLY))
            pl.when(jnp.logical_and(there, far))(functools.partial(act, 2 * EARLY))

    def win_copy(side, turn, to, place, begin):
        slot, rows = 2 * turn + to, HALF - begin
        return remote(
            (to_prev, to_next)[side].at[slot, :, :, pl.ds(begin - EARLY, rows)],
            sides[1 - side][5].at[turn, core, :, :, pl.ds(begin, rows)],
            win_send.at[side, slot], win_recv.at[1 - side, turn, core], (to, place),
        )

    def win_arrival(side, turn, group, place, begin):
        rows = HALF - begin
        return remote(
            to_prev.at[0, :, :, pl.ds(begin - EARLY, rows)], sides[side][5].at[turn, group, :, :, pl.ds(begin, rows)],
            win_send.at[side, 0], win_recv.at[side, turn, group], (core, place),
        )

    def extra_copy(turn, group):
        return remote(
            early_more.at[turn], have_prev.at[turn, group, :, :, pl.ds(EARLY, EARLY)],
            extra_send.at[turn], extra_recv.at[turn], partner,
        )

    def early_copy(side, turn, group):
        return remote(
            (early_prev, early_next)[side].at[turn], sides[side][5].at[turn, group, :, :, pl.ds(0, EARLY)],
            early_send.at[side, turn], early_recv.at[side, turn], partner,
        )

    def part_copy(turn, group):
        return remote(
            to_partner.at[turn], have_own.at[turn, group], part_send.at[turn], part_recv.at[turn], partner
        )

    def grad_copy(side, turn, layer, to, place):
        slot = 2 * turn + core
        return remote(
            top.at[turn, layer], sides[1 - side][6].at[slot, layer % 2],
            grad_send.at[side, turn, layer], grad_recv.at[1 - side, slot, layer % 2], (to, place),
        )

    def grad_arrival(side, slot, part, place):
        return remote(
            top.at[0, 0], sides[side][6].at[slot, part],
            grad_send.at[side, 0, 0], grad_recv.at[side, slot, part], (core, place),
        )

    def detour_copy(side, turn, layer):
        return remote(
            top.at[turn, layer], passed.at[layer % 2], grad_send.at[side, turn, layer], passed_recv.at[layer % 2],
            (core, lat + (DETOUR + 1 if side else -DETOUR - 1)),
        )

    def passed_copy(side, part):
        to, place = (1 - core, lat - DETOUR) if side == 0 else (1 - core, lat + DETOUR)
        return [
            remote(
                passed.at[part], sides[side][6].at[2 + core, part], passed_send.at[part], grad_recv.at[side, 2 + core, part],
                (k, place),
            )
            for k in (core, to)
        ]

    def bottom_copy(turn, part, slot):
        return remote(
            bottom.at[turn, part], own.at[slot, part], bottom_send.at[turn, part], bottom_recv.at[turn, part], partner
        )

    def pos_pass_copy():
        return remote(pos, pos_pass, pass_send.at[0], pass_recv, (core, lat - DETOUR - 1))

    def pos_passed_copies():
        return [
            remote(pos_pass, pos_next, pass_send.at[i], pos_recv.at[1], (k, lat + DETOUR))
            for i, k in enumerate((core, 1 - core))
        ]

    @pl.when(jnp.logical_and(far_prev, first))
    def _():
        pl.semaphore_signal(here_sem, inc=1, device_id=partner, device_id_type=MESH)

    @pl.when(jnp.logical_and(far_prev, second))
    def _():
        pos_pass_copy().start()

    tells = (near_prev, has_next)
    for side, _there, place, *_rest in sides:
        @pl.when(tells[side])
        def _():
            pos_copy(side, place).start()

    for load in loads:
        load.wait()

    @pl.when(jnp.logical_and(far_prev, second))
    def _():
        pl.semaphore_wait(here_sem, 1)

    for side, there, place, *_rest in sides:
        @pl.when(there)
        def _():
            full_copy(side, place).start()

    @pl.when(far_next)
    def _():
        more_copy().start()

    def own_windows(turn, carry):
        have_own[turn, core] = cut(tile, pos, 2 * turn + core, ALL)
        to_partner[turn] = cut(tile, pos, 2 * turn + 1 - core, ALL)
        part_copy(turn, core).start()
        return carry

    lax.fori_loop(0, turns, own_windows, 0)

    for side, there, place, *_rest in sides:
        @pl.when(there)
        def _():
            pos_arrival(side, place).wait_recv()

    @pl.when(jnp.logical_and(passes_down, second))
    def _():
        pos_pass_copy().wait_recv()
        for copy in pos_passed_copies():
            copy.start()

    def send_windows(turn, carry):
        for k in range(2):
            slot = 2 * turn + k
            for side, there, place, where, *_rest in sides:
                @pl.when(there)
                def _():
                    (to_prev, to_next)[side][slot] = cut(tile, where, slot, REST)

                for at_home, to in ((core == k, core), (core != k, 1 - core)):
                    when_near_or_far(
                        side, jnp.logical_and(there, at_home), far_next,
                        lambda begin: win_copy(side, turn, to, place, begin).start(),
                    )

        return carry

    lax.fori_loop(0, turns, send_windows, 0)

    def early_windows(turn, carry):
        for side, there, place, _where, full, have, _arrived in sides:
            @pl.when(there)
            def _():
                have[turn, core, :, :, FIRST] = cut(full, pos, 2 * turn + core, FIRST)
                (early_prev, early_next)[side][turn] = cut(full, pos, 2 * turn + 1 - core, FIRST)
                early_copy(side, turn, core).start()

        return carry

    for side, there, place, *_rest in sides:
        @pl.when(there)
        def _():
            full_arrival(side, place).wait_recv()

    lax.fori_loop(0, turns, early_windows, 0)

    @pl.when(far_prev)
    def _():
        more_arrival().wait_recv()

        def extra_windows(turn, carry):
            have_prev[turn, core, :, :, SECOND] = cut(more_prev, pos, 2 * turn + core, FIRST)
            early_more[turn] = cut(more_prev, pos, 2 * turn + 1 - core, FIRST)
            extra_copy(turn, core).start()
            return carry

        lax.fori_loop(0, turns, extra_windows, 0)

    for load in tables_in:
        load.wait()

    def build_window(turn, group):
        for side, there, place, *_rest in sides:
            when_near_or_far(
                1 - side, there, far_prev, lambda begin: win_arrival(side, turn, group, place, begin).wait_recv()
            )

        @pl.when(core != group)
        def _():
            part_copy(turn, group).wait_recv()
            for side, there, place, *_rest in sides:
                @pl.when(there)
                def _():
                    early_copy(side, turn, group).wait_recv()

            @pl.when(far_prev)
            def _():
                extra_copy(turn, group).wait_recv()

        row = pos[0, 2 * turn + core] - lat * HALF
        rows = lax.broadcasted_iota(jnp.int32, (2, 2, HALF, WIN), 2)
        window[group, :, :, :HALF] = jnp.where(rows >= row, have_prev[turn, group], have_next[turn, group])
        window[group, :, :, HALF:] = have_own[turn, group]

    def times(layer, re, im):
        t_re, t_im = window[layer // 2, 0, layer % 2], window[layer // 2, 1, layer % 2]
        return re * t_re - im * t_im, re * t_im + im * t_re

    def times_conj(layer, re, im):
        t_re, t_im = window[layer // 2, 0, layer % 2], window[layer // 2, 1, layer % 2]
        return re * t_re + im * t_im, im * t_re - re * t_im

    def send_term(turn, layer, re, im):
        p_re, p_im = waves[layer, 0], waves[layer, 1]
        term_re = p_re * re + p_im * im
        term_im = p_re * im - p_im * re
        top[turn, layer, 0] = term_re[:HALF]
        top[turn, layer, 1] = term_im[:HALF]
        slot = 2 * turn + core
        group, part = layer // 2, layer % 2
        for at_home, to in ((core == group, core), (core != group, 1 - core)):
            for side, there, place, *_rest in sides:
                goes = jnp.logical_and(there, at_home)
                if layer in DETOURED:
                    around = jnp.logical_and((far_prev, far_next)[side], turn == 1)

                    @pl.when(jnp.logical_and(goes, around))
                    def _():
                        detour_copy(side, turn, layer).start()

                    goes = jnp.logical_and(goes, jnp.logical_not(around))

                @pl.when(goes)
                def _():
                    grad_copy(side, turn, layer, to, place).start()

        @pl.when(core == group)
        def _():
            own[slot, part, 0] = term_re[HALF:]
            own[slot, part, 1] = term_im[HALF:]

        @pl.when(core != group)
        def _():
            bottom[turn, part, 0] = term_re[HALF:]
            bottom[turn, part, 1] = term_im[HALF:]
            bottom_copy(turn, part, slot).start()

    def whole(turn, carry):
        slot = 2 * turn + core
        row = pos[0, slot] - lat * HALF
        _, lane = column_block(pos, slot)
        re = pltpu.roll(pltpu.roll(probe[0], row, 0), lane, 1)
        im = pltpu.roll(pltpu.roll(probe[1], row, 0), lane, 1)
        for layer in range(4):
            if layer % 2 == 0:
                build_window(turn, layer // 2)
            waves[layer, 0] = re
            waves[layer, 1] = im
            re, im = product(mats, PROP if layer < 3 else DFT, *times(layer, re, im))
        live = jnp.where(slot < counts[0], 1.0, 0.0).astype(jnp.float32)
        weight = live * (1.0 - amp[slot] / jnp.sqrt(re * re + im * im + 1.0))
        re, im = product(mats, DFT_CONJ, weight * re, weight * im)
        for layer in range(3, -1, -1):
            send_term(turn, layer, re, im)
            if layer > 0:
                re, im = product(mats, PROP_CONJ, *times_conj(layer, re, im))
        return carry

    lax.fori_loop(0, turns, whole, 0)

    rows = lax.broadcasted_iota(jnp.int32, (2, HALF, WIN), 1)
    lanes = lax.broadcasted_iota(jnp.int32, (2, HALF, WIN), 2)

    def add(where, slot, part, piece):
        begin = where[1, slot] - HALF
        for k in range(blocks):
            offset = lanes + (k * WIN - begin)
            inside = jnp.logical_and(offset >= 0, offset < WIN)
            grad[:, part, :, k * WIN : (k + 1) * WIN] += jnp.where(inside, piece, 0.0)

    def add_own(turn, carry):
        for k in range(2):
            slot = 2 * turn + k
            for part in range(2):
                @pl.when(core != k)
                def _():
                    bottom_copy(turn, part, slot).wait_recv()

                add(pos, slot, part, own[slot, part])
        return carry

    def add_other(slot, part, side, when):
        _, _there, place, where, _full, _have, arrived = sides[side]

        @pl.when(when)
        def _():
            grad_arrival(side, slot, part, place).wait_recv()
            row = where[0, slot] - place * HALF
            keep = rows < row if side == 0 else rows >= row
            add(where, slot, part, jnp.where(keep, arrived[slot, part], 0.0))

    detoured = [layer % 2 for layer in DETOURED]
    by_detour = [jnp.logical_and(flag, core == 1) for flag in (far_prev, far_next)]

    def add_others(slot, carry):
        for part in (1, 0):
            for side, there, *_rest in sides:
                if part in detoured:
                    there = jnp.logical_and(there, jnp.logical_not(jnp.logical_and(by_detour[side], slot >= 2)))
                add_other(slot, part, side, there)
        return carry

    def add_detoured(slot, carry):
        for part in detoured:
            for side in range(2):
                add_other(slot, part, side, by_detour[side])
        return carry

    lax.fori_loop(0, turns, add_own, 0)
    lax.fori_loop(0, 2, add_others, 0)

    for side, flag in ((0, passes_up), (1, passes_down)):
        for part in [layer % 2 for layer in DETOURED]:
            @pl.when(flag)
            def _():
                pltpu.make_async_remote_copy(
                    src_ref=top.at[0, 0], dst_ref=passed.at[part], send_sem=grad_send.at[side, 0, 0],
                    recv_sem=passed_recv.at[part], device_id=partner, device_id_type=MESH,
                ).wait_recv()

            same, other = passed_copy(side, part)

            @pl.when(jnp.logical_and(flag, core == 1))
            def _():
                same.start()

            @pl.when(jnp.logical_and(flag, core == 0))
            def _():
                other.start()

    for part in (1, 0):
        for from_far in (False, True):
            def add_part(slot, carry):
                for side, there, *_rest in sides:
                    far = (far_prev, far_next)[side]
                    when = far if from_far else jnp.logical_and(there, jnp.logical_not(far))
                    if part in detoured:
                        when = jnp.logical_and(when, jnp.logical_not(by_detour[side]))
                    add_other(slot, part, side, when)
                return carry

            lax.fori_loop(2, slots, add_part, 0)

    if DETOURED:
        lax.fori_loop(2, slots, add_detoured, 0)

    for side, there, place, *_rest in sides:
        @pl.when(there)
        def _():
            full_copy(side, place).wait_send()

        @pl.when(tells[side])
        def _():
            pos_copy(side, place).wait_send()

    @pl.when(jnp.logical_and(far_prev, second))
    def _():
        pos_pass_copy().wait_send()

    @pl.when(jnp.logical_and(passes_down, second))
    def _():
        for copy in pos_passed_copies():
            copy.wait_send()

    @pl.when(far_next)
    def _():
        more_copy().wait_send()

    def finish(turn, carry):
        part_copy(turn, core).wait_send()
        for part in range(2):
            bottom_copy(turn, part, 2 * turn + 1 - core).wait_send()
        for side, there, place, *_rest in sides:
            @pl.when(there)
            def _():
                early_copy(side, turn, core).wait_send()
                for layer in range(4):
                    grad_copy(side, turn, layer, core, place).wait_send()

            for to in (core, 1 - core):
                when_near_or_far(
                    side, there, far_next, lambda begin: win_copy(side, turn, to, place, begin).wait_send()
                )

        @pl.when(far_prev)
        def _():
            extra_copy(turn, core).wait_send()

        return carry

    lax.fori_loop(0, turns, finish, 0)

    @pl.when(passes)
    def _():
        for layer in DETOURED:
            passed_copy(0, layer % 2)[0].wait_send()


def on_device(n, trans, probe, amp, pos, counts):
    slots = pos.shape[0]
    turns = slots // 2
    pos = pos.T
    blocks = trans.shape[3] // WIN
    vmem = pl.BlockSpec(memory_space=pltpu.VMEM)
    hbm = pl.BlockSpec(memory_space=pltpu.HBM)
    f32 = jnp.float32
    piece = (slots, 2, 2, HALF, WIN)
    mats = jnp.asarray(tables())
    held = [pltpu.with_memory_space_constraint(x, pltpu.HBM) for x in (pos, trans, probe, amp, mats)]
    sem = pltpu.SemaphoreType.DMA
    return pl.pallas_call(
        functools.partial(kernel, n),
        out_shape=pltpu.VMEM(trans.shape, f32),
        in_specs=[hbm] * 6,
        out_specs=vmem,
        scratch_shapes=[
            pltpu.VMEM((blocks + 2, 2, 2, HALF, WIN), f32),
            pltpu.VMEM(probe.shape, f32),
            pltpu.VMEM(amp.shape, f32),
            pltpu.VMEM(mats.shape, jnp.bfloat16),
            pltpu.VMEM((blocks + 2, 2, 2, EARLY, WIN), f32),
            pltpu.VMEM((blocks + 2, 2, 2, EARLY, WIN), f32),
            pltpu.VMEM((blocks + 2, 2, 2, EARLY, WIN), f32),
            pltpu.VMEM((slots, 2, 2, HALF - EARLY, WIN), f32),
            pltpu.VMEM((slots, 2, 2, HALF - EARLY, WIN), f32),
            pltpu.VMEM((turns, 2, 2, HALF, WIN), f32),
            pltpu.VMEM((turns, 2, 2, EARLY, WIN), f32),
            pltpu.VMEM((turns, 2, 2, EARLY, WIN), f32),
            pltpu.VMEM((turns, 2, 2, EARLY, WIN), f32),
            pltpu.VMEM((turns, 2, 2, 2, HALF, WIN), f32),
            pltpu.VMEM((turns, 2, 2, 2, HALF, WIN), f32),
            pltpu.VMEM((turns, 2, 2, 2, HALF, WIN), f32),
            pltpu.VMEM(piece, f32),
            pltpu.VMEM(piece, f32),
            pltpu.VMEM(piece, f32),
            pltpu.VMEM((2, 2, 2, WIN, WIN), f32),
            pltpu.VMEM((4, 2, WIN, WIN), f32),
            pltpu.VMEM((turns, 4, 2, HALF, WIN), f32),
            pltpu.VMEM((turns, 2, 2, HALF, WIN), f32),
            pltpu.VMEM((2, 2, HALF, WIN), f32),
            pltpu.SMEM(pos.shape, jnp.int32),
            pltpu.SMEM(counts.shape, jnp.int32),
            pltpu.SMEM(pos.shape, jnp.int32),
            pltpu.SMEM(pos.shape, jnp.int32),
            pltpu.SMEM(pos.shape, jnp.int32),
            pltpu.SemaphoreType.REGULAR,
            sem((blocks,)),
            sem((3,)),
            sem((2,)),
            sem((2,)),
            sem((2,)),
            sem((2,)),
            sem((2,)),
            sem((2, turns)),
            sem((2, turns)),
            sem(()),
            sem(()),
            sem((turns,)),
            sem((turns,)),
            sem((turns,)),
            sem((turns,)),
            sem((2, slots)),
            sem((2, turns, 2)),
            sem((2, turns, 4)),
            sem((2, slots, 2)),
            sem((turns, 2)),
            sem((turns, 2)),
            sem((2,)),
            sem((2,)),
            sem((2,)),
            sem(()),
        ],
        compiler_params=pltpu.CompilerParams(
            collective_id=0, has_side_effects=True, vmem_limit_bytes=40 << 20
        ),
        name="windows",
    )(held[0], counts, *held[1:])


def solution(mesh):
    placed = (P(None, "depth", "lat", None), P(), P("lat", None, None), P("lat", None), P("lat"))
    return jax.shard_map(
        functools.partial(on_device, mesh.shape["lat"]),
        mesh=mesh,
        in_specs=placed,
        out_specs=P(None, "depth", "lat", None),
        check_vma=False,
    )
```

```python
import functools

import jax
import jax.numpy as jnp
import ml_dtypes
import numpy as np
from jax import lax
from jax.experimental import pallas as pl
from jax.experimental.pallas import tpu as pltpu
from jax.sharding import PartitionSpec as P

PROP_COEF = 40.0
WIN = 128
HALF = 64
EARLY = 8
PLANE = 16
DETOUR = 3
MESH = pl.DeviceIdType.MESH
PROP, PROP_CONJ, DFT, DFT_CONJ = range(4)


def tables():
    index = np.arange(WIN)
    dft = np.exp(-2j * np.pi * (np.outer(index, index) % WIN) / WIN) / np.sqrt(WIN)
    freq = ((index + WIN // 2) % WIN - WIN // 2) / WIN
    prop = dft.conj() @ np.diag(np.exp(-1j * PROP_COEF * freq * freq)) @ dft
    terms = []
    for matrix in (prop, prop.conj(), dft, dft.conj()):
        real = np.block([[matrix.real, -matrix.imag], [matrix.imag, matrix.real]])
        high = real.astype(ml_dtypes.bfloat16)
        low = (real - high.astype(np.float64)).astype(ml_dtypes.bfloat16)
        terms.append(np.stack([high, low]))
    return np.stack(terms)


def split(values):
    high = values.astype(jnp.bfloat16)
    low = (values - high.astype(jnp.float32)).astype(jnp.bfloat16)
    return high, low


def product(mats, which, re, im):
    conj = which ^ 1
    high, low = split(jnp.concatenate([re, im], axis=1))
    right = jnp.concatenate([mats[conj, 0], mats[conj, 0], mats[conj, 1]], axis=0)
    first = jnp.dot(
        jnp.concatenate([high, low, high], axis=1), right, preferred_element_type=jnp.float32
    )
    high, low = split(first)
    left = jnp.concatenate(
        [mats[which, 0, :, :WIN], mats[which, 0, :, :WIN], mats[which, 1, :, :WIN]], axis=1
    )
    second = jnp.dot(
        left, jnp.concatenate([high, low, high], axis=0), preferred_element_type=jnp.float32
    )
    return second[:WIN, :WIN] - second[WIN:, WIN:], second[:WIN, WIN:] + second[WIN:, :WIN]


def column_block(pos, slot):
    column = pos[1, slot] + HALF
    return lax.shift_right_logical(column, 7), column & (WIN - 1)


def cut(tile, pos, slot, rows):
    block, lane = column_block(pos, slot)
    first, second = tile[block, :, :, rows], tile[block + 1, :, :, rows]
    lanes = lax.broadcasted_iota(jnp.int32, first.shape, 3)
    return jnp.where(lanes >= lane, first, second)


DETOURED = (3,)
ALL = slice(0, HALF)
FIRST = slice(0, EARLY)
REST = slice(EARLY, HALF)


def kernel(
    n, pos_hbm, counts_hbm, trans, probe_hbm, amp_hbm, mats_hbm,
    grad,
    tile, probe, amp, mats, full_prev, full_next, to_prev, to_next, to_partner, early_prev, early_next,
    have_prev, have_next, have_own, from_prev, from_next, own, window, waves, top, bottom, passed, pos, counts, pos_prev, pos_next, pos_pass,
    here_sem, tile_sem, table_sem, pos_sem, pos_send, pos_recv, full_send, full_recv, early_send, early_recv,
    part_send, part_recv, win_send, win_recv, grad_send, grad_recv, bottom_send, bottom_recv, passed_send, passed_recv, pass_send, pass_recv,
):
    core = lax.axis_index("depth")
    lat = lax.axis_index("lat")
    has_prev = lat > 0
    has_next = lat < n - 1
    far_prev = jnp.logical_and(has_prev, lax.rem(lat, PLANE) == 0)
    far_next = jnp.logical_and(has_next, lax.rem(lat, PLANE) == PLANE - 1)
    first_of_plane, last_of_plane = lat - DETOUR, lat + DETOUR
    passes_up = jnp.logical_and(first_of_plane > 0, lax.rem(first_of_plane, PLANE) == 0)
    passes_down = jnp.logical_and(last_of_plane < n - 1, lax.rem(last_of_plane, PLANE) == PLANE - 1)
    passes = jnp.logical_or(passes_up, passes_down)
    slots = pos.shape[1]
    turns = slots // 2
    blocks = tile.shape[0] - 2
    partner = (1 - core, lat)
    sides = (
        (0, has_prev, lat - 1, pos_prev, full_prev, have_prev, from_prev),
        (1, has_next, lat + 1, pos_next, full_next, have_next, from_next),
    )

    scalars = [
        pltpu.make_async_copy(source, target, pos_sem.at[k])
        for k, (source, target) in enumerate(((pos_hbm, pos), (counts_hbm, counts)))
    ]
    loads = [
        pltpu.make_async_copy(
            trans.at[:, :, :, pl.ds(k * WIN, WIN)], tile.at[k + 1], tile_sem.at[k]
        )
        for k in range(blocks)
    ]
    tables_in = [
        pltpu.make_async_copy(source, target, table_sem.at[k])
        for k, (source, target) in enumerate(((mats_hbm, mats), (probe_hbm, probe), (amp_hbm, amp)))
    ]
    for load in scalars + loads + tables_in:
        load.start()

    barrier = pltpu.get_barrier_semaphore()
    near_prev = jnp.logical_and(has_prev, jnp.logical_not(far_prev))
    near_next = jnp.logical_and(has_next, jnp.logical_not(far_next))
    first, second = core == 0, core == 1
    to_same = ((has_prev, lat - 1), (jnp.logical_or(near_next, jnp.logical_and(far_next, first)), lat + 1))
    to_other = ((has_prev, lat - 1), (jnp.logical_or(near_next, jnp.logical_and(far_next, second)), lat + 1))
    for targets, k in ((to_same, core), (to_other, 1 - core)):
        for there, place in targets:
            @pl.when(there)
            def _():
                pl.semaphore_signal(barrier, inc=1, device_id=(k, place), device_id_type=MESH)

    pl.semaphore_signal(barrier, inc=1, device_id=partner, device_id_type=MESH)

    @pl.when(passes_up)
    def _():
        pl.semaphore_signal(barrier, inc=1, device_id=(core, lat - DETOUR - 1), device_id_type=MESH)

    @pl.when(passes_down)
    def _():
        pl.semaphore_signal(barrier, inc=1, device_id=(core, lat + DETOUR + 1), device_id_type=MESH)

    @pl.when(jnp.logical_and(far_next, first))
    def _():
        pl.semaphore_signal(barrier, inc=1, device_id=(1 - core, lat - DETOUR), device_id_type=MESH)

    for flag, place in ((far_prev, lat + DETOUR), (far_next, lat - DETOUR)):
        @pl.when(jnp.logical_and(flag, core == 1))
        def _():
            for k in (core, 1 - core):
                pl.semaphore_signal(barrier, inc=1, device_id=(k, place), device_id_type=MESH)

    grad[...] = jnp.zeros_like(grad)
    for padded in (tile, full_prev, full_next):
        padded[0] = jnp.zeros(padded.shape[1:], jnp.float32)
        padded[blocks + 1] = jnp.zeros(padded.shape[1:], jnp.float32)
    for _, there, _place, where, full, have, _arrived in sides:
        @pl.when(jnp.logical_not(there))
        def _():
            have[...] = jnp.zeros_like(have)
            for k in range(slots):
                where[0, k] = 0
                where[1, k] = 0

    for load in scalars:
        load.wait()
    pl.semaphore_wait(
        barrier,
        1 + 2 * jnp.logical_or(near_prev, jnp.logical_and(far_prev, first)).astype(jnp.int32)
        + 2 * has_next.astype(jnp.int32) + jnp.logical_and(passes_down, second).astype(jnp.int32)
        + far_prev.astype(jnp.int32) + far_next.astype(jnp.int32) + passes.astype(jnp.int32),
    )

    def remote(source, target, send, recv, device):
        return pltpu.make_async_remote_copy(
            src_ref=source, dst_ref=target, send_sem=send, recv_sem=recv,
            device_id=device, device_id_type=MESH,
        )

    def pos_copy(side, place):
        return remote(pos, sides[1 - side][3], pos_send.at[side], pos_recv.at[1 - side], (core, place))

    def pos_arrival(side, place):
        return remote(pos, sides[side][3], pos_send.at[side], pos_recv.at[side], (core, place))

    def full_copy(side, place):
        return remote(
            tile.at[pl.ds(1, blocks), :, :, pl.ds(0, EARLY)], sides[1 - side][4].at[pl.ds(1, blocks)],
            full_send.at[side], full_recv.at[1 - side], (core, place),
        )

    def full_arrival(side, place):
        return remote(
            tile.at[pl.ds(1, blocks), :, :, pl.ds(0, EARLY)], sides[side][4].at[pl.ds(1, blocks)],
            full_send.at[side], full_recv.at[side], (core, place),
        )

    def win_copy(side, turn, to, place):
        slot = 2 * turn + to
        return remote(
            (to_prev, to_next)[side].at[slot], sides[1 - side][5].at[turn, core, :, :, pl.ds(EARLY, HALF - EARLY)],
            win_send.at[side, slot], win_recv.at[1 - side, turn, core], (to, place),
        )

    def win_arrival(side, turn, group, place):
        return remote(
            to_prev.at[0], sides[side][5].at[turn, group, :, :, pl.ds(EARLY, HALF - EARLY)],
            win_send.at[side, 0], win_recv.at[side, turn, group], (core, place),
        )

    def early_copy(side, turn, group):
        return remote(
            (early_prev, early_next)[side].at[turn], sides[side][5].at[turn, group, :, :, pl.ds(0, EARLY)],
            early_send.at[side, turn], early_recv.at[side, turn], partner,
        )

    def part_copy(turn, group):
        return remote(
            to_partner.at[turn], have_own.at[turn, group], part_send.at[turn], part_recv.at[turn], partner
        )

    def grad_copy(side, turn, layer, to, place):
        slot = 2 * turn + core
        return remote(
            top.at[turn, layer], sides[1 - side][6].at[slot, layer % 2],
            grad_send.at[side, turn, layer], grad_recv.at[1 - side, slot, layer % 2], (to, place),
        )

    def grad_arrival(side, slot, part, place):
        return remote(
            top.at[0, 0], sides[side][6].at[slot, part],
            grad_send.at[side, 0, 0], grad_recv.at[side, slot, part], (core, place),
        )

    def detour_copy(side, turn, layer):
        return remote(
            top.at[turn, layer], passed.at[layer % 2], grad_send.at[side, turn, layer], passed_recv.at[layer % 2],
            (core, lat + (DETOUR + 1 if side else -DETOUR - 1)),
        )

    def passed_copy(side, part):
        to, place = (1 - core, lat - DETOUR) if side == 0 else (1 - core, lat + DETOUR)
        return [
            remote(
                passed.at[part], sides[side][6].at[2 + core, part], passed_send.at[part], grad_recv.at[side, 2 + core, part],
                (k, place),
            )
            for k in (core, to)
        ]

    def bottom_copy(turn, part, slot):
        return remote(
            bottom.at[turn, part], own.at[slot, part], bottom_send.at[turn, part], bottom_recv.at[turn, part], partner
        )

    def pos_pass_copy():
        return remote(pos, pos_pass, pass_send.at[0], pass_recv, (core, lat - DETOUR - 1))

    def pos_passed_copies():
        return [
            remote(pos_pass, pos_next, pass_send.at[i], pos_recv.at[1], (k, lat + DETOUR))
            for i, k in enumerate((core, 1 - core))
        ]

    @pl.when(jnp.logical_and(far_prev, first))
    def _():
        pl.semaphore_signal(here_sem, inc=1, device_id=partner, device_id_type=MESH)

    @pl.when(jnp.logical_and(far_prev, second))
    def _():
        pos_pass_copy().start()

    tells = (near_prev, has_next)
    for side, _there, place, *_rest in sides:
        @pl.when(tells[side])
        def _():
            pos_copy(side, place).start()

    for load in loads:
        load.wait()

    @pl.when(jnp.logical_and(far_prev, second))
    def _():
        pl.semaphore_wait(here_sem, 1)

    for side, there, place, *_rest in sides:
        @pl.when(there)
        def _():
            full_copy(side, place).start()

    def own_windows(turn, carry):
        have_own[turn, core] = cut(tile, pos, 2 * turn + core, ALL)
        to_partner[turn] = cut(tile, pos, 2 * turn + 1 - core, ALL)
        part_copy(turn, core).start()
        return carry

    lax.fori_loop(0, turns, own_windows, 0)

    for side, there, place, *_rest in sides:
        @pl.when(there)
        def _():
            pos_arrival(side, place).wait_recv()

    @pl.when(jnp.logical_and(passes_down, second))
    def _():
        pos_pass_copy().wait_recv()
        for copy in pos_passed_copies():
            copy.start()

    def send_windows(turn, carry):
        for k in range(2):
            slot = 2 * turn + k
            for side, there, place, where, *_rest in sides:
                @pl.when(there)
                def _():
                    (to_prev, to_next)[side][slot] = cut(tile, where, slot, REST)

                for at_home, to in ((core == k, core), (core != k, 1 - core)):
                    @pl.when(jnp.logical_and(there, at_home))
                    def _():
                        win_copy(side, turn, to, place).start()

        return carry

    lax.fori_loop(0, turns, send_windows, 0)

    def early_windows(turn, carry):
        for side, there, place, _where, full, have, _arrived in sides:
            @pl.when(there)
            def _():
                have[turn, core, :, :, FIRST] = cut(full, pos, 2 * turn + core, FIRST)
                (early_prev, early_next)[side][turn] = cut(full, pos, 2 * turn + 1 - core, FIRST)
                early_copy(side, turn, core).start()

        return carry

    for side, there, place, *_rest in sides:
        @pl.when(there)
        def _():
            full_arrival(side, place).wait_recv()

    lax.fori_loop(0, turns, early_windows, 0)

    for load in tables_in:
        load.wait()

    def build_window(turn, group):
        for side, there, place, *_rest in sides:
            @pl.when(there)
            def _():
                win_arrival(side, turn, group, place).wait_recv()

        @pl.when(core != group)
        def _():
            part_copy(turn, group).wait_recv()
            for side, there, place, *_rest in sides:
                @pl.when(there)
                def _():
                    early_copy(side, turn, group).wait_recv()

        row = pos[0, 2 * turn + core] - lat * HALF
        rows = lax.broadcasted_iota(jnp.int32, (2, 2, HALF, WIN), 2)
        window[group, :, :, :HALF] = jnp.where(rows >= row, have_prev[turn, group], have_next[turn, group])
        window[group, :, :, HALF:] = have_own[turn, group]

    def times(layer, re, im):
        t_re, t_im = window[layer // 2, 0, layer % 2], window[layer // 2, 1, layer % 2]
        return re * t_re - im * t_im, re * t_im + im * t_re

    def times_conj(layer, re, im):
        t_re, t_im = window[layer // 2, 0, layer % 2], window[layer // 2, 1, layer % 2]
        return re * t_re + im * t_im, im * t_re - re * t_im

    def send_term(turn, layer, re, im):
        p_re, p_im = waves[layer, 0], waves[layer, 1]
        term_re = p_re * re + p_im * im
        term_im = p_re * im - p_im * re
        top[turn, layer, 0] = term_re[:HALF]
        top[turn, layer, 1] = term_im[:HALF]
        slot = 2 * turn + core
        group, part = layer // 2, layer % 2
        for at_home, to in ((core == group, core), (core != group, 1 - core)):
            for side, there, place, *_rest in sides:
                goes = jnp.logical_and(there, at_home)
                if layer in DETOURED:
                    around = jnp.logical_and((far_prev, far_next)[side], turn == 1)

                    @pl.when(jnp.logical_and(goes, around))
                    def _():
                        detour_copy(side, turn, layer).start()

                    goes = jnp.logical_and(goes, jnp.logical_not(around))

                @pl.when(goes)
                def _():
                    grad_copy(side, turn, layer, to, place).start()

        @pl.when(core == group)
        def _():
            own[slot, part, 0] = term_re[HALF:]
            own[slot, part, 1] = term_im[HALF:]

        @pl.when(core != group)
        def _():
            bottom[turn, part, 0] = term_re[HALF:]
            bottom[turn, part, 1] = term_im[HALF:]
            bottom_copy(turn, part, slot).start()

    def whole(turn, carry):
        slot = 2 * turn + core
        row = pos[0, slot] - lat * HALF
        _, lane = column_block(pos, slot)
        re = pltpu.roll(pltpu.roll(probe[0], row, 0), lane, 1)
        im = pltpu.roll(pltpu.roll(probe[1], row, 0), lane, 1)
        for layer in range(4):
            if layer % 2 == 0:
                build_window(turn, layer // 2)
            waves[layer, 0] = re
            waves[layer, 1] = im
            re, im = product(mats, PROP if layer < 3 else DFT, *times(layer, re, im))
        live = jnp.where(slot < counts[0], 1.0, 0.0).astype(jnp.float32)
        weight = live * (1.0 - amp[slot] / jnp.sqrt(re * re + im * im + 1.0))
        re, im = product(mats, DFT_CONJ, weight * re, weight * im)
        for layer in range(3, -1, -1):
            send_term(turn, layer, re, im)
            if layer > 0:
                re, im = product(mats, PROP_CONJ, *times_conj(layer, re, im))
        return carry

    lax.fori_loop(0, turns, whole, 0)

    rows = lax.broadcasted_iota(jnp.int32, (2, HALF, WIN), 1)
    lanes = lax.broadcasted_iota(jnp.int32, (2, HALF, WIN), 2)

    def add(where, slot, part, piece):
        begin = where[1, slot] - HALF
        for k in range(blocks):
            offset = lanes + (k * WIN - begin)
            inside = jnp.logical_and(offset >= 0, offset < WIN)
            grad[:, part, :, k * WIN : (k + 1) * WIN] += jnp.where(inside, piece, 0.0)

    def add_own(turn, carry):
        for k in range(2):
            slot = 2 * turn + k
            for part in range(2):
                @pl.when(core != k)
                def _():
                    bottom_copy(turn, part, slot).wait_recv()

                add(pos, slot, part, own[slot, part])
        return carry

    def add_other(slot, part, side, when):
        _, _there, place, where, _full, _have, arrived = sides[side]

        @pl.when(when)
        def _():
            grad_arrival(side, slot, part, place).wait_recv()
            row = where[0, slot] - place * HALF
            keep = rows < row if side == 0 else rows >= row
            add(where, slot, part, jnp.where(keep, arrived[slot, part], 0.0))

    detoured = [layer % 2 for layer in DETOURED]
    by_detour = [jnp.logical_and(flag, core == 1) for flag in (far_prev, far_next)]

    def add_others(slot, carry):
        for part in (1, 0):
            for side, there, *_rest in sides:
                if part in detoured:
                    there = jnp.logical_and(there, jnp.logical_not(jnp.logical_and(by_detour[side], slot >= 2)))
                add_other(slot, part, side, there)
        return carry

    def add_detoured(slot, carry):
        for part in detoured:
            for side in range(2):
                add_other(slot, part, side, by_detour[side])
        return carry

    lax.fori_loop(0, turns, add_own, 0)
    lax.fori_loop(0, 2, add_others, 0)

    for side, flag in ((0, passes_up), (1, passes_down)):
        for part in [layer % 2 for layer in DETOURED]:
            @pl.when(flag)
            def _():
                pltpu.make_async_remote_copy(
                    src_ref=top.at[0, 0], dst_ref=passed.at[part], send_sem=grad_send.at[side, 0, 0],
                    recv_sem=passed_recv.at[part], device_id=partner, device_id_type=MESH,
                ).wait_recv()

            same, other = passed_copy(side, part)

            @pl.when(jnp.logical_and(flag, core == 1))
            def _():
                same.start()

            @pl.when(jnp.logical_and(flag, core == 0))
            def _():
                other.start()

    for part in (1, 0):
        for from_far in (False, True):
            def add_part(slot, carry):
                for side, there, *_rest in sides:
                    far = (far_prev, far_next)[side]
                    when = far if from_far else jnp.logical_and(there, jnp.logical_not(far))
                    if part in detoured:
                        when = jnp.logical_and(when, jnp.logical_not(by_detour[side]))
                    add_other(slot, part, side, when)
                return carry

            lax.fori_loop(2, slots, add_part, 0)

    if DETOURED:
        lax.fori_loop(2, slots, add_detoured, 0)

    for side, there, place, *_rest in sides:
        @pl.when(there)
        def _():
            full_copy(side, place).wait_send()

        @pl.when(tells[side])
        def _():
            pos_copy(side, place).wait_send()

    @pl.when(jnp.logical_and(far_prev, second))
    def _():
        pos_pass_copy().wait_send()

    @pl.when(jnp.logical_and(passes_down, second))
    def _():
        for copy in pos_passed_copies():
            copy.wait_send()

    def finish(turn, carry):
        part_copy(turn, core).wait_send()
        for part in range(2):
            bottom_copy(turn, part, 2 * turn + 1 - core).wait_send()
        for side, there, place, *_rest in sides:
            @pl.when(there)
            def _():
                early_copy(side, turn, core).wait_send()
                for layer in range(4):
                    grad_copy(side, turn, layer, core, place).wait_send()
                for to in (core, 1 - core):
                    win_copy(side, turn, to, place).wait_send()

        return carry

    lax.fori_loop(0, turns, finish, 0)

    @pl.when(passes)
    def _():
        for layer in DETOURED:
            passed_copy(0, layer % 2)[0].wait_send()


def on_device(n, trans, probe, amp, pos, counts):
    slots = pos.shape[0]
    turns = slots // 2
    pos = pos.T
    blocks = trans.shape[3] // WIN
    vmem = pl.BlockSpec(memory_space=pltpu.VMEM)
    hbm = pl.BlockSpec(memory_space=pltpu.HBM)
    f32 = jnp.float32
    piece = (slots, 2, 2, HALF, WIN)
    mats = jnp.asarray(tables())
    held = [pltpu.with_memory_space_constraint(x, pltpu.HBM) for x in (pos, trans, probe, amp, mats)]
    sem = pltpu.SemaphoreType.DMA
    return pl.pallas_call(
        functools.partial(kernel, n),
        out_shape=pltpu.VMEM(trans.shape, f32),
        in_specs=[hbm] * 6,
        out_specs=vmem,
        scratch_shapes=[
            pltpu.VMEM((blocks + 2, 2, 2, HALF, WIN), f32),
            pltpu.VMEM(probe.shape, f32),
            pltpu.VMEM(amp.shape, f32),
            pltpu.VMEM(mats.shape, jnp.bfloat16),
            pltpu.VMEM((blocks + 2, 2, 2, EARLY, WIN), f32),
            pltpu.VMEM((blocks + 2, 2, 2, EARLY, WIN), f32),
            pltpu.VMEM((slots, 2, 2, HALF - EARLY, WIN), f32),
            pltpu.VMEM((slots, 2, 2, HALF - EARLY, WIN), f32),
            pltpu.VMEM((turns, 2, 2, HALF, WIN), f32),
            pltpu.VMEM((turns, 2, 2, EARLY, WIN), f32),
            pltpu.VMEM((turns, 2, 2, EARLY, WIN), f32),
            pltpu.VMEM((turns, 2, 2, 2, HALF, WIN), f32),
            pltpu.VMEM((turns, 2, 2, 2, HALF, WIN), f32),
            pltpu.VMEM((turns, 2, 2, 2, HALF, WIN), f32),
            pltpu.VMEM(piece, f32),
            pltpu.VMEM(piece, f32),
            pltpu.VMEM(piece, f32),
            pltpu.VMEM((2, 2, 2, WIN, WIN), f32),
            pltpu.VMEM((4, 2, WIN, WIN), f32),
            pltpu.VMEM((turns, 4, 2, HALF, WIN), f32),
            pltpu.VMEM((turns, 2, 2, HALF, WIN), f32),
            pltpu.VMEM((2, 2, HALF, WIN), f32),
            pltpu.SMEM(pos.shape, jnp.int32),
            pltpu.SMEM(counts.shape, jnp.int32),
            pltpu.SMEM(pos.shape, jnp.int32),
            pltpu.SMEM(pos.shape, jnp.int32),
            pltpu.SMEM(pos.shape, jnp.int32),
            pltpu.SemaphoreType.REGULAR,
            sem((blocks,)),
            sem((3,)),
            sem((2,)),
            sem((2,)),
            sem((2,)),
            sem((2,)),
            sem((2,)),
            sem((2, turns)),
            sem((2, turns)),
            sem((turns,)),
            sem((turns,)),
            sem((2, slots)),
            sem((2, turns, 2)),
            sem((2, turns, 4)),
            sem((2, slots, 2)),
            sem((turns, 2)),
            sem((turns, 2)),
            sem((2,)),
            sem((2,)),
            sem((2,)),
            sem(()),
        ],
        compiler_params=pltpu.CompilerParams(
            collective_id=0, has_side_effects=True, vmem_limit_bytes=40 << 20
        ),
        name="windows",
    )(held[0], counts, *held[1:])


def solution(mesh):
    placed = (P(None, "depth", "lat", None), P(), P("lat", None, None), P("lat", None), P("lat"))
    return jax.shard_map(
        functools.partial(on_device, mesh.shape["lat"]),
        mesh=mesh,
        in_specs=placed,
        out_specs=P(None, "depth", "lat", None),
        check_vma=False,
    )
```

```python
import functools

import jax
import jax.numpy as jnp
import ml_dtypes
import numpy as np
from jax import lax
from jax.experimental import pallas as pl
from jax.experimental.pallas import tpu as pltpu
from jax.sharding import PartitionSpec as P

PROP_COEF = 40.0
WIN = 128
HALF = 64
EARLY = 8
PLANE = 16
DETOUR = 3
MESH = pl.DeviceIdType.MESH
PROP, PROP_CONJ, DFT, DFT_CONJ = range(4)


def tables():
    index = np.arange(WIN)
    dft = np.exp(-2j * np.pi * (np.outer(index, index) % WIN) / WIN) / np.sqrt(WIN)
    freq = ((index + WIN // 2) % WIN - WIN // 2) / WIN
    prop = dft.conj() @ np.diag(np.exp(-1j * PROP_COEF * freq * freq)) @ dft
    terms = []
    for matrix in (prop, prop.conj(), dft, dft.conj()):
        real = np.block([[matrix.real, -matrix.imag], [matrix.imag, matrix.real]])
        high = real.astype(ml_dtypes.bfloat16)
        low = (real - high.astype(np.float64)).astype(ml_dtypes.bfloat16)
        terms.append(np.stack([high, low]))
    return np.stack(terms)


def split(values):
    high = values.astype(jnp.bfloat16)
    low = (values - high.astype(jnp.float32)).astype(jnp.bfloat16)
    return high, low


def product(mats, which, re, im):
    conj = which ^ 1
    high, low = split(jnp.concatenate([re, im], axis=1))
    right = jnp.concatenate([mats[conj, 0], mats[conj, 0], mats[conj, 1]], axis=0)
    first = jnp.dot(
        jnp.concatenate([high, low, high], axis=1), right, preferred_element_type=jnp.float32
    )
    high, low = split(first)
    left = jnp.concatenate(
        [mats[which, 0, :, :WIN], mats[which, 0, :, :WIN], mats[which, 1, :, :WIN]], axis=1
    )
    second = jnp.dot(
        left, jnp.concatenate([high, low, high], axis=0), preferred_element_type=jnp.float32
    )
    return second[:WIN, :WIN] - second[WIN:, WIN:], second[:WIN, WIN:] + second[WIN:, :WIN]


def column_block(pos, slot):
    column = pos[1, slot] + HALF
    return lax.shift_right_logical(column, 7), column & (WIN - 1)


def cut(tile, pos, slot, rows):
    block, lane = column_block(pos, slot)
    first, second = tile[block, :, :, rows], tile[block + 1, :, :, rows]
    lanes = lax.broadcasted_iota(jnp.int32, first.shape, 3)
    return jnp.where(lanes >= lane, first, second)


DETOURED = (3,)
ALL = slice(0, HALF)
FIRST = slice(0, EARLY)
SECOND = slice(EARLY, 2 * EARLY)
REST = slice(EARLY, HALF)


def kernel(
    n, pos_hbm, counts_hbm, trans, probe_hbm, amp_hbm, mats_hbm,
    grad,
    tile, probe, amp, mats, full_prev, full_next, more_prev, to_prev, to_next, to_partner, early_prev, early_next, early_more,
    have_prev, have_next, have_own, from_prev, from_next, own, window, waves, top, bottom, passed, pos, counts, pos_prev, pos_next, pos_pass,
    here_sem, tile_sem, table_sem, pos_sem, pos_send, pos_recv, full_send, full_recv, early_send, early_recv,
    more_send, more_recv, extra_send, extra_recv,
    part_send, part_recv, win_send, win_recv, grad_send, grad_recv, bottom_send, bottom_recv, passed_send, passed_recv, pass_send, pass_recv,
):
    core = lax.axis_index("depth")
    lat = lax.axis_index("lat")
    has_prev = lat > 0
    has_next = lat < n - 1
    far_prev = jnp.logical_and(has_prev, lax.rem(lat, PLANE) == 0)
    far_next = jnp.logical_and(has_next, lax.rem(lat, PLANE) == PLANE - 1)
    first_of_plane, last_of_plane = lat - DETOUR, lat + DETOUR
    passes_up = jnp.logical_and(first_of_plane > 0, lax.rem(first_of_plane, PLANE) == 0)
    passes_down = jnp.logical_and(last_of_plane < n - 1, lax.rem(last_of_plane, PLANE) == PLANE - 1)
    passes = jnp.logical_or(passes_up, passes_down)
    slots = pos.shape[1]
    turns = slots // 2
    blocks = tile.shape[0] - 2
    partner = (1 - core, lat)
    sides = (
        (0, has_prev, lat - 1, pos_prev, full_prev, have_prev, from_prev),
        (1, has_next, lat + 1, pos_next, full_next, have_next, from_next),
    )

    scalars = [
        pltpu.make_async_copy(source, target, pos_sem.at[k])
        for k, (source, target) in enumerate(((pos_hbm, pos), (counts_hbm, counts)))
    ]
    loads = [
        pltpu.make_async_copy(
            trans.at[:, :, :, pl.ds(k * WIN, WIN)], tile.at[k + 1], tile_sem.at[k]
        )
        for k in range(blocks)
    ]
    tables_in = [
        pltpu.make_async_copy(source, target, table_sem.at[k])
        for k, (source, target) in enumerate(((mats_hbm, mats), (probe_hbm, probe), (amp_hbm, amp)))
    ]
    for load in scalars + loads + tables_in:
        load.start()

    barrier = pltpu.get_barrier_semaphore()
    near_prev = jnp.logical_and(has_prev, jnp.logical_not(far_prev))
    near_next = jnp.logical_and(has_next, jnp.logical_not(far_next))
    first, second = core == 0, core == 1
    to_same = ((has_prev, lat - 1), (jnp.logical_or(near_next, jnp.logical_and(far_next, first)), lat + 1))
    to_other = ((has_prev, lat - 1), (jnp.logical_or(near_next, jnp.logical_and(far_next, second)), lat + 1))
    for targets, k in ((to_same, core), (to_other, 1 - core)):
        for there, place in targets:
            @pl.when(there)
            def _():
                pl.semaphore_signal(barrier, inc=1, device_id=(k, place), device_id_type=MESH)

    pl.semaphore_signal(barrier, inc=1, device_id=partner, device_id_type=MESH)

    @pl.when(passes_up)
    def _():
        pl.semaphore_signal(barrier, inc=1, device_id=(core, lat - DETOUR - 1), device_id_type=MESH)

    @pl.when(passes_down)
    def _():
        pl.semaphore_signal(barrier, inc=1, device_id=(core, lat + DETOUR + 1), device_id_type=MESH)

    @pl.when(jnp.logical_and(far_next, first))
    def _():
        pl.semaphore_signal(barrier, inc=1, device_id=(1 - core, lat - DETOUR), device_id_type=MESH)

    for flag, place in ((far_prev, lat + DETOUR), (far_next, lat - DETOUR)):
        @pl.when(jnp.logical_and(flag, core == 1))
        def _():
            for k in (core, 1 - core):
                pl.semaphore_signal(barrier, inc=1, device_id=(k, place), device_id_type=MESH)

    grad[...] = jnp.zeros_like(grad)
    for padded in (tile, full_prev, full_next, more_prev):
        padded[0] = jnp.zeros(padded.shape[1:], jnp.float32)
        padded[blocks + 1] = jnp.zeros(padded.shape[1:], jnp.float32)
    for _, there, _place, where, full, have, _arrived in sides:
        @pl.when(jnp.logical_not(there))
        def _():
            have[...] = jnp.zeros_like(have)
            for k in range(slots):
                where[0, k] = 0
                where[1, k] = 0

    for load in scalars:
        load.wait()
    pl.semaphore_wait(
        barrier,
        1 + 2 * jnp.logical_or(near_prev, jnp.logical_and(far_prev, first)).astype(jnp.int32)
        + 2 * has_next.astype(jnp.int32) + jnp.logical_and(passes_down, second).astype(jnp.int32)
        + far_prev.astype(jnp.int32) + far_next.astype(jnp.int32) + passes.astype(jnp.int32),
    )

    def remote(source, target, send, recv, device):
        return pltpu.make_async_remote_copy(
            src_ref=source, dst_ref=target, send_sem=send, recv_sem=recv,
            device_id=device, device_id_type=MESH,
        )

    def pos_copy(side, place):
        return remote(pos, sides[1 - side][3], pos_send.at[side], pos_recv.at[1 - side], (core, place))

    def pos_arrival(side, place):
        return remote(pos, sides[side][3], pos_send.at[side], pos_recv.at[side], (core, place))

    def full_copy(side, place):
        return remote(
            tile.at[pl.ds(1, blocks), :, :, pl.ds(0, EARLY)], sides[1 - side][4].at[pl.ds(1, blocks)],
            full_send.at[side], full_recv.at[1 - side], (core, place),
        )

    def full_arrival(side, place):
        return remote(
            tile.at[pl.ds(1, blocks), :, :, pl.ds(0, EARLY)], sides[side][4].at[pl.ds(1, blocks)],
            full_send.at[side], full_recv.at[side], (core, place),
        )

    def more_copy():
        return remote(
            tile.at[pl.ds(1, blocks), :, :, pl.ds(EARLY, EARLY)], more_prev.at[pl.ds(1, blocks)],
            more_send, more_recv, (core, lat + 1),
        )

    def more_arrival():
        return remote(
            tile.at[pl.ds(1, blocks), :, :, pl.ds(EARLY, EARLY)], more_prev.at[pl.ds(1, blocks)],
            more_send, more_recv, (core, lat - 1),
        )

    def when_near_or_far(side, there, far, act):
        if side == 0:
            pl.when(there)(functools.partial(act, EARLY))
        else:
            pl.when(jnp.logical_and(there, jnp.logical_not(far)))(functools.partial(act, EARLY))
            pl.when(jnp.logical_and(there, far))(functools.partial(act, 2 * EARLY))

    def win_copy(side, turn, to, place, begin):
        slot, rows = 2 * turn + to, HALF - begin
        return remote(
            (to_prev, to_next)[side].at[slot, :, :, pl.ds(begin - EARLY, rows)],
            sides[1 - side][5].at[turn, core, :, :, pl.ds(begin, rows)],
            win_send.at[side, slot], win_recv.at[1 - side, turn, core], (to, place),
        )

    def win_arrival(side, turn, group, place, begin):
        rows = HALF - begin
        return remote(
            to_prev.at[0, :, :, pl.ds(begin - EARLY, rows)], sides[side][5].at[turn, group, :, :, pl.ds(begin, rows)],
            win_send.at[side, 0], win_recv.at[side, turn, group], (core, place),
        )

    def extra_copy(turn, group):
        return remote(
            early_more.at[turn], have_prev.at[turn, group, :, :, pl.ds(EARLY, EARLY)],
            extra_send.at[turn], extra_recv.at[turn], partner,
        )

    def early_copy(side, turn, group):
        return remote(
            (early_prev, early_next)[side].at[turn], sides[side][5].at[turn, group, :, :, pl.ds(0, EARLY)],
            early_send.at[side, turn], early_recv.at[side, turn], partner,
        )

    def part_copy(turn, group):
        return remote(
            to_partner.at[turn], have_own.at[turn, group], part_send.at[turn], part_recv.at[turn], partner
        )

    def grad_copy(side, turn, layer, to, place):
        slot = 2 * turn + core
        return remote(
            top.at[turn, layer], sides[1 - side][6].at[slot, layer % 2],
            grad_send.at[side, turn, layer], grad_recv.at[1 - side, slot, layer % 2], (to, place),
        )

    def grad_arrival(side, slot, part, place):
        return remote(
            top.at[0, 0], sides[side][6].at[slot, part],
            grad_send.at[side, 0, 0], grad_recv.at[side, slot, part], (core, place),
        )

    def detour_copy(side, turn, layer):
        return remote(
            top.at[turn, layer], passed.at[layer % 2], grad_send.at[side, turn, layer], passed_recv.at[layer % 2],
            (core, lat + (DETOUR + 1 if side else -DETOUR - 1)),
        )

    def passed_copy(side, part):
        to, place = (1 - core, lat - DETOUR) if side == 0 else (1 - core, lat + DETOUR)
        return [
            remote(
                passed.at[part], sides[side][6].at[2 + core, part], passed_send.at[part], grad_recv.at[side, 2 + core, part],
                (k, place),
            )
            for k in (core, to)
        ]

    def bottom_copy(turn, part, slot):
        return remote(
            bottom.at[turn, part], own.at[slot, part], bottom_send.at[turn, part], bottom_recv.at[turn, part], partner
        )

    def pos_pass_copy():
        return remote(pos, pos_pass, pass_send.at[0], pass_recv, (core, lat - DETOUR - 1))

    def pos_passed_copies():
        return [
            remote(pos_pass, pos_next, pass_send.at[i], pos_recv.at[1], (k, lat + DETOUR))
            for i, k in enumerate((core, 1 - core))
        ]

    @pl.when(jnp.logical_and(far_prev, first))
    def _():
        pl.semaphore_signal(here_sem, inc=1, device_id=partner, device_id_type=MESH)

    @pl.when(jnp.logical_and(far_prev, second))
    def _():
        pos_pass_copy().start()

    tells = (near_prev, has_next)
    for side, _there, place, *_rest in sides:
        @pl.when(tells[side])
        def _():
            pos_copy(side, place).start()

    for load in loads:
        load.wait()

    @pl.when(jnp.logical_and(far_prev, second))
    def _():
        pl.semaphore_wait(here_sem, 1)

    for side, there, place, *_rest in sides:
        @pl.when(there)
        def _():
            full_copy(side, place).start()

    @pl.when(far_next)
    def _():
        more_copy().start()

    def own_windows(turn, carry):
        have_own[turn, core] = cut(tile, pos, 2 * turn + core, ALL)
        to_partner[turn] = cut(tile, pos, 2 * turn + 1 - core, ALL)
        part_copy(turn, core).start()
        return carry

    lax.fori_loop(0, turns, own_windows, 0)

    for side, there, place, *_rest in sides:
        @pl.when(there)
        def _():
            pos_arrival(side, place).wait_recv()

    @pl.when(jnp.logical_and(passes_down, second))
    def _():
        pos_pass_copy().wait_recv()
        for copy in pos_passed_copies():
            copy.start()

    def send_windows(turn, carry):
        for k in range(2):
            slot = 2 * turn + k
            for side, there, place, where, *_rest in sides:
                @pl.when(there)
                def _():
                    (to_prev, to_next)[side][slot] = cut(tile, where, slot, REST)

                for at_home, to in ((core == k, core), (core != k, 1 - core)):
                    when_near_or_far(
                        side, jnp.logical_and(there, at_home), far_next,
                        lambda begin: win_copy(side, turn, to, place, begin).start(),
                    )

        return carry

    lax.fori_loop(0, turns, send_windows, 0)

    def early_windows(turn, carry):
        for side, there, place, _where, full, have, _arrived in sides:
            @pl.when(there)
            def _():
                have[turn, core, :, :, FIRST] = cut(full, pos, 2 * turn + core, FIRST)
                (early_prev, early_next)[side][turn] = cut(full, pos, 2 * turn + 1 - core, FIRST)
                early_copy(side, turn, core).start()

        return carry

    for side, there, place, *_rest in sides:
        @pl.when(there)
        def _():
            full_arrival(side, place).wait_recv()

    lax.fori_loop(0, turns, early_windows, 0)

    @pl.when(far_prev)
    def _():
        more_arrival().wait_recv()

        def extra_windows(turn, carry):
            have_prev[turn, core, :, :, SECOND] = cut(more_prev, pos, 2 * turn + core, FIRST)
            early_more[turn] = cut(more_prev, pos, 2 * turn + 1 - core, FIRST)
            extra_copy(turn, core).start()
            return carry

        lax.fori_loop(0, turns, extra_windows, 0)

    for load in tables_in:
        load.wait()

    def build_window(turn, group):
        for side, there, place, *_rest in sides:
            when_near_or_far(
                1 - side, there, far_prev, lambda begin: win_arrival(side, turn, group, place, begin).wait_recv()
            )

        @pl.when(core != group)
        def _():
            part_copy(turn, group).wait_recv()
            for side, there, place, *_rest in sides:
                @pl.when(there)
                def _():
                    early_copy(side, turn, group).wait_recv()

            @pl.when(far_prev)
            def _():
                extra_copy(turn, group).wait_recv()

        row = pos[0, 2 * turn + core] - lat * HALF
        rows = lax.broadcasted_iota(jnp.int32, (2, 2, HALF, WIN), 2)
        window[group, :, :, :HALF] = jnp.where(rows >= row, have_prev[turn, group], have_next[turn, group])
        window[group, :, :, HALF:] = have_own[turn, group]

    def times(layer, re, im):
        t_re, t_im = window[layer // 2, 0, layer % 2], window[layer // 2, 1, layer % 2]
        return re * t_re - im * t_im, re * t_im + im * t_re

    def times_conj(layer, re, im):
        t_re, t_im = window[layer // 2, 0, layer % 2], window[layer // 2, 1, layer % 2]
        return re * t_re + im * t_im, im * t_re - re * t_im

    def send_term(turn, layer, re, im):
        p_re, p_im = waves[layer, 0], waves[layer, 1]
        term_re = p_re * re + p_im * im
        term_im = p_re * im - p_im * re
        top[turn, layer, 0] = term_re[:HALF]
        top[turn, layer, 1] = term_im[:HALF]
        slot = 2 * turn + core
        group, part = layer // 2, layer % 2
        for at_home, to in ((core == group, core), (core != group, 1 - core)):
            for side, there, place, *_rest in sides:
                goes = jnp.logical_and(there, at_home)
                if layer in DETOURED:
                    around = jnp.logical_and((far_prev, far_next)[side], turn == 1)

                    @pl.when(jnp.logical_and(goes, around))
                    def _():
                        detour_copy(side, turn, layer).start()

                    goes = jnp.logical_and(goes, jnp.logical_not(around))

                @pl.when(goes)
                def _():
                    grad_copy(side, turn, layer, to, place).start()

        @pl.when(core == group)
        def _():
            own[slot, part, 0] = term_re[HALF:]
            own[slot, part, 1] = term_im[HALF:]

        @pl.when(core != group)
        def _():
            bottom[turn, part, 0] = term_re[HALF:]
            bottom[turn, part, 1] = term_im[HALF:]
            bottom_copy(turn, part, slot).start()

    def whole(turn, carry):
        slot = 2 * turn + core
        row = pos[0, slot] - lat * HALF
        _, lane = column_block(pos, slot)
        re = pltpu.roll(pltpu.roll(probe[0], row, 0), lane, 1)
        im = pltpu.roll(pltpu.roll(probe[1], row, 0), lane, 1)
        for layer in range(4):
            if layer % 2 == 0:
                build_window(turn, layer // 2)
            waves[layer, 0] = re
            waves[layer, 1] = im
            re, im = product(mats, PROP if layer < 3 else DFT, *times(layer, re, im))
        live = jnp.where(slot < counts[0], 1.0, 0.0).astype(jnp.float32)
        weight = live * (1.0 - amp[slot] / jnp.sqrt(re * re + im * im + 1.0))
        re, im = product(mats, DFT_CONJ, weight * re, weight * im)
        for layer in range(3, -1, -1):
            send_term(turn, layer, re, im)
            if layer > 0:
                re, im = product(mats, PROP_CONJ, *times_conj(layer, re, im))
        return carry

    lax.fori_loop(0, turns, whole, 0)

    for side, flag in ((0, passes_up), (1, passes_down)):
        for part in [layer % 2 for layer in DETOURED]:
            @pl.when(flag)
            def _():
                pltpu.make_async_remote_copy(
                    src_ref=top.at[0, 0], dst_ref=passed.at[part], send_sem=grad_send.at[side, 0, 0],
                    recv_sem=passed_recv.at[part], device_id=partner, device_id_type=MESH,
                ).wait_recv()

            same, other = passed_copy(side, part)

            @pl.when(jnp.logical_and(flag, core == 1))
            def _():
                same.start()

            @pl.when(jnp.logical_and(flag, core == 0))
            def _():
                other.start()

    rows = lax.broadcasted_iota(jnp.int32, (2, HALF, WIN), 1)
    lanes = lax.broadcasted_iota(jnp.int32, (2, HALF, WIN), 2)

    def add(where, slot, part, piece):
        begin = where[1, slot] - HALF
        for k in range(blocks):
            offset = lanes + (k * WIN - begin)
            inside = jnp.logical_and(offset >= 0, offset < WIN)
            grad[:, part, :, k * WIN : (k + 1) * WIN] += jnp.where(inside, piece, 0.0)

    def add_own(turn, carry):
        for k in range(2):
            slot = 2 * turn + k
            for part in range(2):
                @pl.when(core != k)
                def _():
                    bottom_copy(turn, part, slot).wait_recv()

                add(pos, slot, part, own[slot, part])
        return carry

    def add_other(slot, part, side, when):
        _, _there, place, where, _full, _have, arrived = sides[side]

        @pl.when(when)
        def _():
            grad_arrival(side, slot, part, place).wait_recv()
            row = where[0, slot] - place * HALF
            keep = rows < row if side == 0 else rows >= row
            add(where, slot, part, jnp.where(keep, arrived[slot, part], 0.0))

    detoured = [layer % 2 for layer in DETOURED]
    by_detour = [jnp.logical_and(flag, core == 1) for flag in (far_prev, far_next)]

    def add_others(slot, carry):
        for part in (1, 0):
            for side, there, *_rest in sides:
                if part in detoured:
                    there = jnp.logical_and(there, jnp.logical_not(jnp.logical_and(by_detour[side], slot >= 2)))
                add_other(slot, part, side, there)
        return carry

    def add_detoured(slot, carry):
        for part in detoured:
            for side in range(2):
                add_other(slot, part, side, by_detour[side])
        return carry

    lax.fori_loop(0, turns, add_own, 0)
    lax.fori_loop(0, 2, add_others, 0)

    for part in (1, 0):
        for from_far in (False, True):
            def add_part(slot, carry):
                for side, there, *_rest in sides:
                    far = (far_prev, far_next)[side]
                    when = far if from_far else jnp.logical_and(there, jnp.logical_not(far))
                    if part in detoured:
                        when = jnp.logical_and(when, jnp.logical_not(by_detour[side]))
                    add_other(slot, part, side, when)
                return carry

            lax.fori_loop(2, slots, add_part, 0)

    if DETOURED:
        lax.fori_loop(2, slots, add_detoured, 0)

    for side, there, place, *_rest in sides:
        @pl.when(there)
        def _():
            full_copy(side, place).wait_send()

        @pl.when(tells[side])
        def _():
            pos_copy(side, place).wait_send()

    @pl.when(jnp.logical_and(far_prev, second))
    def _():
        pos_pass_copy().wait_send()

    @pl.when(jnp.logical_and(passes_down, second))
    def _():
        for copy in pos_passed_copies():
            copy.wait_send()

    @pl.when(far_next)
    def _():
        more_copy().wait_send()

    def finish(turn, carry):
        part_copy(turn, core).wait_send()
        for part in range(2):
            bottom_copy(turn, part, 2 * turn + 1 - core).wait_send()
        for side, there, place, *_rest in sides:
            @pl.when(there)
            def _():
                early_copy(side, turn, core).wait_send()
                for layer in range(4):
                    grad_copy(side, turn, layer, core, place).wait_send()

            for to in (core, 1 - core):
                when_near_or_far(
                    side, there, far_next, lambda begin: win_copy(side, turn, to, place, begin).wait_send()
                )

        @pl.when(far_prev)
        def _():
            extra_copy(turn, core).wait_send()

        return carry

    lax.fori_loop(0, turns, finish, 0)

    @pl.when(passes)
    def _():
        for layer in DETOURED:
            passed_copy(0, layer % 2)[0].wait_send()


def on_device(n, trans, probe, amp, pos, counts):
    slots = pos.shape[0]
    turns = slots // 2
    pos = pos.T
    blocks = trans.shape[3] // WIN
    vmem = pl.BlockSpec(memory_space=pltpu.VMEM)
    hbm = pl.BlockSpec(memory_space=pltpu.HBM)
    f32 = jnp.float32
    piece = (slots, 2, 2, HALF, WIN)
    mats = jnp.asarray(tables())
    held = [pltpu.with_memory_space_constraint(x, pltpu.HBM) for x in (pos, trans, probe, amp, mats)]
    sem = pltpu.SemaphoreType.DMA
    return pl.pallas_call(
        functools.partial(kernel, n),
        out_shape=pltpu.VMEM(trans.shape, f32),
        in_specs=[hbm] * 6,
        out_specs=vmem,
        scratch_shapes=[
            pltpu.VMEM((blocks + 2, 2, 2, HALF, WIN), f32),
            pltpu.VMEM(probe.shape, f32),
            pltpu.VMEM(amp.shape, f32),
            pltpu.VMEM(mats.shape, jnp.bfloat16),
            pltpu.VMEM((blocks + 2, 2, 2, EARLY, WIN), f32),
            pltpu.VMEM((blocks + 2, 2, 2, EARLY, WIN), f32),
            pltpu.VMEM((blocks + 2, 2, 2, EARLY, WIN), f32),
            pltpu.VMEM((slots, 2, 2, HALF - EARLY, WIN), f32),
            pltpu.VMEM((slots, 2, 2, HALF - EARLY, WIN), f32),
            pltpu.VMEM((turns, 2, 2, HALF, WIN), f32),
            pltpu.VMEM((turns, 2, 2, EARLY, WIN), f32),
            pltpu.VMEM((turns, 2, 2, EARLY, WIN), f32),
            pltpu.VMEM((turns, 2, 2, EARLY, WIN), f32),
            pltpu.VMEM((turns, 2, 2, 2, HALF, WIN), f32),
            pltpu.VMEM((turns, 2, 2, 2, HALF, WIN), f32),
            pltpu.VMEM((turns, 2, 2, 2, HALF, WIN), f32),
            pltpu.VMEM(piece, f32),
            pltpu.VMEM(piece, f32),
            pltpu.VMEM(piece, f32),
            pltpu.VMEM((2, 2, 2, WIN, WIN), f32),
            pltpu.VMEM((4, 2, WIN, WIN), f32),
            pltpu.VMEM((turns, 4, 2, HALF, WIN), f32),
            pltpu.VMEM((turns, 2, 2, HALF, WIN), f32),
            pltpu.VMEM((2, 2, HALF, WIN), f32),
            pltpu.SMEM(pos.shape, jnp.int32),
            pltpu.SMEM(counts.shape, jnp.int32),
            pltpu.SMEM(pos.shape, jnp.int32),
            pltpu.SMEM(pos.shape, jnp.int32),
            pltpu.SMEM(pos.shape, jnp.int32),
            pltpu.SemaphoreType.REGULAR,
            sem((blocks,)),
            sem((3,)),
            sem((2,)),
            sem((2,)),
            sem((2,)),
            sem((2,)),
            sem((2,)),
            sem((2, turns)),
            sem((2, turns)),
            sem(()),
            sem(()),
            sem((turns,)),
            sem((turns,)),
            sem((turns,)),
            sem((turns,)),
            sem((2, slots)),
            sem((2, turns, 2)),
            sem((2, turns, 4)),
            sem((2, slots, 2)),
            sem((turns, 2)),
            sem((turns, 2)),
            sem((2,)),
            sem((2,)),
            sem((2,)),
            sem(()),
        ],
        compiler_params=pltpu.CompilerParams(
            collective_id=0, has_side_effects=True, vmem_limit_bytes=40 << 20
        ),
        name="windows",
    )(held[0], counts, *held[1:])


def solution(mesh):
    placed = (P(None, "depth", "lat", None), P(), P("lat", None, None), P("lat", None), P("lat"))
    return jax.shard_map(
        functools.partial(on_device, mesh.shape["lat"]),
        mesh=mesh,
        in_specs=placed,
        out_specs=P(None, "depth", "lat", None),
        check_vma=False,
    )
```
